32 devices in a mesh: section: 4 (over y, x), tp: 8 (over z, core).
Axes of the slice: x: 2, y: 2, z: 4, core: 2. Of those that a mesh axis runs over, the one named last changes fastest.
Arguments:
- tokens: bfloat16 [64, 8192], P(None, 'tp'), may hold values from -6 to 6
- norm_gain: float32 [4, 8192], P('section'), may hold values from 0.1 to 1.9
- gate_weight: bfloat16 [4, 8192, 16384], P('section', None, 'tp'), may hold values from -0.09375 to 0.09375
- up_weight: bfloat16 [4, 8192, 16384], P('section', None, 'tp'), may hold values from -0.09375 to 0.09375
- gate_mask: int32 [4, 128, 256], P('section', None, 'tp'), may hold values 0 or 1
- up_mask: int32 [4, 128, 256], P('section', None, 'tp'), may hold values 0 or 1
- down_weight: bfloat16 [4, 16384, 8192], P('section', 'tp'), may hold values from -0.125 to 0.125
- down_mask: int32 [4, 256, 128], P('section', 'tp'), may hold values 0 or 1
- slot_order: int32 [4, 256], P('section', 'tp'), may hold values from 0 to 255, as said below
Outputs:
- received: bfloat16 [4, 64, 8192], P('section', None, 'tp')
The draws below stay inside these ranges and needn't reach their ends.
Inputs may be any that keep to these rules, and one draw needn't show every extreme that they name: `slot_order`: for each section a permutation of the 256 hidden blocks. Slot k lies on tp device k // 32; block b is computed on tp device b // 32. The slots of tp device t take exactly 4 blocks from each of the tp devices t, t + 1, ..., t + 8 - 1 (mod 8) and none from others. `gate_mask`: 1 keeps a block, 0 prunes it. `up_mask`: 1 keeps a block, 0 prunes it. `down_mask`: 1 keeps a block, 0 prunes it.
All inputs are finite; a program needn't handle non-finite values.
Results may differ from the reference program's by a relative error of at most 0.014.
Values may be sent and summed in bfloat16 or wider, within the bound.
No kernel may reach another device: no remote copies, remote signals or barrier semaphores. Data moves between devices by JAX's collectives and lax.ppermute only.
A program may use at most 320 MiB of HBM per device.

```python
import jax
import jax.numpy as jnp
from jax import lax

D = 8192
FF = 16384
BLOCK = 64
ROWS = 64
NB = 256
BLK_DEV = 32
N_SECTION = 4
N_TP = 8


def draw_slot_order(key, part):
    window = min(N_TP, BLK_DEV)
    capacity = BLK_DEV // window

    def single(section_key):
        first_key, second_key = jax.random.split(section_key)
        given = jax.vmap(lambda sub_key: jax.random.permutation(sub_key, BLK_DEV))(jax.random.split(first_key, N_TP))
        lanes = jax.vmap(lambda sub_key: jax.random.permutation(sub_key, BLK_DEV))(jax.random.split(second_key, N_TP))
        target = jnp.arange(N_TP, dtype=jnp.int32)[:, None]
        offset = (lanes // capacity).astype(jnp.int32)
        source = (target + offset) % N_TP
        local_block = given[source, lanes]
        return (source * BLK_DEV + local_block).reshape(-1).astype(jnp.int32)
    return jax.vmap(single)(jax.random.split(key, N_SECTION))


def touch_ends(result, key, least, top_value):
    shape = result.shape
    index_at = [jax.random.randint(jax.random.fold_in(key, axis), (), 0, shape[axis]) for axis in range(len(shape))]
    result = result.at[tuple(index_at)].set(least)
    longest = shape.index(max(shape))
    index_at[longest] = (index_at[longest] + 1) % shape[longest]
    return result.at[tuple(index_at)].set(top_value)


def shard_levels(stream_key, dims, cuts, low, top_value):
    def one(axis_at, parts):
        heights = jax.random.uniform(jax.random.fold_in(jax.random.fold_in(stream_key, 6), axis_at), (parts,), jnp.float32, low / len(cuts), top_value / len(cuts))
        return jnp.repeat(jnp.exp(heights), dims[axis_at] // parts).reshape((-1,) + (1,) * (len(dims) - axis_at - 1))

    factor_of = one(*cuts[0])
    for cut in cuts[1:]:
        factor_of = factor_of * one(*cut)
    return factor_of


def noise(own_key, dims, width, most, cuts=(), kind=jnp.bfloat16):
    array = width * jax.random.normal(own_key, dims, jnp.float32)
    if cuts:
        array = array * shard_levels(own_key, dims, cuts, -0.22, 0.18)
    return jnp.clip(array, -most, most).astype(kind)


def setup_inputs(seed: int = 0) -> dict:
    streams_of = jax.random.split(jax.random.key(seed), 10)
    return {
        "tokens": noise(streams_of[0], (ROWS, D), 1.0, 6.0, ((1, 8),)),
        "norm_gain": jnp.clip(1.0 + 0.18 * jax.random.normal(streams_of[1], (N_SECTION, D), jnp.float32), 0.1, 1.9),
        "gate_weight": noise(streams_of[2], (N_SECTION, D, FF), (D // 2) ** -0.5, 0.09375, ((0, 4), (2, 8))),
        "up_weight": noise(streams_of[3], (N_SECTION, D, FF), (D // 2) ** -0.5, 0.09375, ((0, 4), (2, 8))),
        "gate_mask": touch_ends((jax.random.randint(streams_of[4], (N_SECTION, D // BLOCK, NB), 0, 2) < 1).astype(jnp.int32), jax.random.fold_in(streams_of[4], 1), 0, 1),
        "up_mask": touch_ends((jax.random.randint(streams_of[5], (N_SECTION, D // BLOCK, NB), 0, 2) < 1).astype(jnp.int32), jax.random.fold_in(streams_of[5], 1), 0, 1),
        "down_weight": noise(streams_of[6], (N_SECTION, FF, D), (FF // 8) ** -0.5, 0.125, ((0, 4), (1, 8))),
        "down_mask": touch_ends((jax.random.randint(streams_of[7], (N_SECTION, NB, D // BLOCK), 0, 2) < 1).astype(jnp.int32), jax.random.fold_in(streams_of[7], 1), 0, 1),
        "slot_order": draw_slot_order(jax.random.fold_in(streams_of[9], 71), 0),
    }


def expand_mask(mask):
    return jnp.repeat(jnp.repeat(mask, BLOCK, axis=0), BLOCK, axis=1)

def masked(weight, mask):
    return weight * expand_mask(mask).astype(jnp.bfloat16)

def layer(inputs, gain, gate_weight, up_weight, gate_mask, up_mask, down_weight, down_mask, order):
    widened = inputs.astype(jnp.float32)
    scale = jax.lax.rsqrt(lax.optimization_barrier(jnp.mean(widened * widened, axis=-1, keepdims=True)) + 1e-05)
    normed = (widened * scale * gain).astype(jnp.bfloat16)
    gate = jnp.dot(normed, masked(gate_weight, gate_mask), preferred_element_type=jnp.float32)
    upper = jnp.dot(normed, masked(up_weight, up_mask), preferred_element_type=jnp.float32)
    hidden = (jax.nn.silu(gate) * upper).astype(jnp.bfloat16)
    tiles = hidden.reshape(ROWS, NB, BLOCK)[:, order.astype(jnp.int32), :].reshape(ROWS, FF)
    summed = jnp.dot(tiles, masked(down_weight, down_mask), preferred_element_type=jnp.float32)
    return (widened + summed).astype(jnp.bfloat16)

def reference(tokens, norm_gain, gate_weight, up_weight, gate_mask, up_mask, down_weight, down_mask, slot_order):
    current = tokens
    results = [None] * N_SECTION
    for layer_pos in range(N_SECTION):
        current = layer(current, norm_gain[layer_pos], gate_weight[layer_pos], up_weight[layer_pos], gate_mask[layer_pos], up_mask[layer_pos], down_weight[layer_pos], down_mask[layer_pos], slot_order[layer_pos])
        results[(layer_pos + 1) % N_SECTION] = current
    return jnp.stack(results)
```

```python
import functools

import jax
import jax.numpy as jnp
from jax import lax
from jax.experimental import pallas as pl
from jax.experimental.pallas import tpu as pltpu
from jax.sharding import PartitionSpec as P


def passed_along(block, axis, distance):
    devices = range(lax.axis_size(axis))
    route = [((i - distance) % len(devices), i) for i in devices]
    return lax.ppermute(block, axis, route)


def expand_mask(mask, width):
    return jnp.repeat(jnp.repeat(mask, width, axis=0), width, axis=1)


def masked(weight, mask, width):
    return weight * expand_mask(mask, width).astype(jnp.bfloat16)


def ring_body(
    tokens,
    norm_gain,
    gate_weight,
    up_weight,
    gate_mask,
    up_mask,
    down_weight,
    down_mask,
    slot_order,
):
    sections = lax.axis_size("section")
    tp_count = lax.axis_size("tp")
    section_pos = lax.axis_index("section")
    tp_pos = lax.axis_index("tp")
    width = gate_weight.shape[1] // gate_mask.shape[1]
    w_gate = masked(gate_weight[0], gate_mask[0], width)
    w_up = masked(up_weight[0], up_mask[0], width)
    w_down = masked(down_weight[0], down_mask[0], width)
    gain = norm_gain[0]
    my_blocks = slot_order[0]
    per_device = my_blocks.shape[0]
    row_count, own_cols = tokens.shape
    window = min(tp_count, per_device)
    capacity = per_device // window
    slot_ids = jnp.arange(capacity, dtype=jnp.int32)
    my_source = my_blocks // per_device
    my_offset = (my_source - tp_pos) % tp_count
    lanes = jnp.arange(per_device, dtype=jnp.int32)
    earlier = (my_source[None, :] == my_source[:, None]) & (lanes[None, :] < lanes[:, None])
    my_rank = jnp.sum(earlier.astype(jnp.int32), axis=1)
    send_lists = []
    for offset in range(window):
        if offset == 0:
            table_row = my_blocks
        else:
            table_row = passed_along(my_blocks, "tp", offset)
        row_source = table_row // per_device
        row_block = table_row % per_device
        from_me = (row_source == tp_pos).astype(jnp.int32)
        order_rank = jnp.cumsum(from_me) - 1
        picks = (from_me[None, :] == 1) & (order_rank[None, :] == slot_ids[:, None])
        send_lists.append(jnp.sum(jnp.where(picks, row_block[None, :], 0), axis=1))
    x_full = lax.all_gather(tokens, "tp", axis=1, tiled=True)
    saved = jnp.zeros((row_count, own_cols), jnp.bfloat16)
    for round_pos in range(sections):
        x_own = lax.dynamic_slice_in_dim(x_full, tp_pos * own_cols, own_cols, 1)
        widened = x_full.astype(jnp.float32)
        scale = lax.rsqrt(jnp.mean(widened * widened, axis=-1, keepdims=True) + 1e-05)
        normed = (widened * scale * gain).astype(jnp.bfloat16)
        gate = jnp.dot(normed, w_gate, preferred_element_type=jnp.float32)
        upper = jnp.dot(normed, w_up, preferred_element_type=jnp.float32)
        hidden = (jax.nn.silu(gate) * upper).astype(jnp.bfloat16)
        flat = (
            hidden.reshape(row_count, per_device, width)
            .transpose(1, 0, 2)
            .reshape(per_device, row_count * width)
        )
        arrivals = []
        for gather_offset in range(window):
            outgoing = flat[send_lists[gather_offset]]
            if gather_offset == 0:
                arrivals.append(outgoing)
            else:
                arrivals.append(passed_along(outgoing, "tp", tp_count - gather_offset))
        stacked = jnp.stack(arrivals)
        chosen = stacked[my_offset, my_rank]
        mine = (
            chosen.reshape(per_device, row_count, width)
            .transpose(1, 0, 2)
            .reshape(row_count, per_device * width)
        )
        partial_sum = jnp.dot(mine, w_down, preferred_element_type=jnp.float32)
        summed = lax.psum_scatter(partial_sum, "tp", scatter_dimension=1, tiled=True)
        y_own = (x_own.astype(jnp.float32) + summed).astype(jnp.bfloat16)
        got_own = passed_along(y_own, "section", 1)
        if round_pos + 1 < sections:
            x_full = lax.all_gather(got_own, "tp", axis=1, tiled=True)
        saved = jnp.where(section_pos == (round_pos + 1) % sections, got_own, saved)
    return saved[None]


BF = jnp.bfloat16
F32 = jnp.float32
VM = pl.BlockSpec(memory_space=pltpu.VMEM)
SM = pl.BlockSpec(memory_space=pltpu.SMEM)
HB = pl.BlockSpec(memory_space=pl.ANY)
MIB = 2**20


def place(load_pair, first, second):
    lanes = lax.broadcasted_iota(jnp.int32, (1, 128), 1)
    left = pltpu.roll(load_pair(first // 2), 64 * (first % 2), 1)
    right = pltpu.roll(load_pair(second // 2), 64 * (1 - second % 2), 1)
    return jnp.where(lanes < 64, left, right).astype(BF)


def gate_up_kernel(
    tile, slots, me_ref, send_ref, x_ref, gain_ref, gm_ref, um_ref, wg, wu, out_ref,
    buf, sem, normed, masks, acc,
):
    pieces, rows, cols = x_ref.shape
    depth, hid = wg.shape[1], wg.shape[2]
    blocks = gm_ref.shape[1]
    width = hid // blocks
    per = cols // tile
    steps = pieces * per
    kept = tile // width
    me = me_ref[0]

    def source(piece):
        half = pieces // 2
        return me ^ (piece // half + 2 * (piece % half))

    def start_row(step):
        return pl.multiple_of(source(step // per) * cols + (step % per) * tile, tile)

    def copies(step, slot):
        return [
            pltpu.make_async_copy(
                w.at[0, pl.ds(start_row(step), tile)], buf.at[slot, j], sem.at[slot, j]
            )
            for j, w in enumerate((wg, wu))
        ]

    for step in range(slots):
        for copy in copies(step, step):
            copy.start()
    spread = (
        lax.broadcasted_iota(jnp.int32, (blocks, hid), 0)
        == lax.broadcasted_iota(jnp.int32, (blocks, hid), 1) // width
    ).astype(BF)
    for j, mask in enumerate((gm_ref, um_ref)):
        masks[j] = jnp.dot(mask[...].astype(F32).astype(BF), spread, preferred_element_type=F32)
    total = jnp.zeros((rows, 1), F32)
    for piece in range(pieces):
        wide = x_ref[piece].astype(F32)
        total = total + jnp.sum(wide * wide, axis=1, keepdims=True)
    scale = lax.rsqrt(total / depth + 1e-05)
    for piece in range(pieces):
        gain = gain_ref[:, pl.ds(pl.multiple_of(source(piece) * cols, cols), cols)]
        normed[piece] = (x_ref[piece].astype(F32) * scale * gain).astype(BF)
    acc[...] = jnp.zeros_like(acc)

    def step_body(step, carry):
        slot = lax.rem(step, slots)
        part = pl.multiple_of((step % per) * tile, tile)
        x_part = normed[step // per, :, pl.ds(part, tile)]
        mask_row = pl.multiple_of(start_row(step) // width, kept)
        for j, copy in enumerate(copies(step, slot)):
            copy.wait()
            mask = masks[j, pl.ds(mask_row, kept), :].astype(BF)
            weight = (buf[slot, j].reshape(kept, width, hid) * mask[:, None, :]).reshape(tile, hid)
            acc[j] += jnp.dot(x_part, weight, preferred_element_type=F32)

        @pl.when(step + slots < steps)
        def _():
            for copy in copies(step + slots, slot):
                copy.start()

        return carry

    lax.fori_loop(0, steps, step_body, 0)
    gate = acc[0]
    hidden = (gate / (1.0 + jnp.exp(-gate)) * acc[1]).astype(BF)
    acc[0] = hidden.astype(F32)

    def load_pair(pair):
        return acc[0, :, pl.ds(pl.multiple_of(pair * 128, 128), 128)]

    each = out_ref.shape[2] // 128
    for piece in range(pieces):
        for pair in range(each):
            at = piece * 2 * each + 2 * pair
            out_ref[piece, :, pl.ds(pair * 128, 128)] = place(
                load_pair, send_ref[at], send_ref[at + 1]
            )


def gate_up(me, send, x, gain, gate_mask, up_mask, w_gate, w_up):
    pieces, rows, cols = x.shape
    depth, hid = w_gate.shape[1:]
    tile, slots = 512, 4
    return pl.pallas_call(
        functools.partial(gate_up_kernel, tile, slots),
        in_specs=[SM, SM, VM, VM, VM, VM, HB, HB],
        out_specs=VM,
        out_shape=jax.ShapeDtypeStruct((pieces, rows, hid // pieces), BF),
        scratch_shapes=[
            pltpu.VMEM((slots, 2, tile, hid), BF),
            pltpu.SemaphoreType.DMA((slots, 2)),
            pltpu.VMEM((pieces, rows, cols), BF),
            pltpu.VMEM((2, gate_mask.shape[0], hid), F32),
            pltpu.VMEM((2, rows, hid), F32),
        ],
        compiler_params=pltpu.CompilerParams(vmem_limit_bytes=32 * MIB),
        cost_estimate=pl.CostEstimate(
            flops=4 * rows * depth * hid, bytes_accessed=4 * depth * hid, transcendentals=0
        ),
        name="gate_up",
    )(me, send, x, gain, gate_mask, up_mask, w_gate, w_up)


def down_kernel(
    tile, slots, me_ref, take_ref, arrived, x_ref, mask_ref, wd, keep_ref, pass_ref,
    buf, sem, mine,
):
    pieces, rows, share = arrived.shape
    hid = wd.shape[1]
    cols = wd.shape[2] // pieces
    blocks, out_blocks = mask_ref.shape
    width = hid // blocks
    per = cols // tile
    steps = pieces * per
    half = pieces // 2
    me = me_ref[0]

    def start_col(step):
        piece = step // per
        target = me ^ ((1 - piece // half) + 2 * (piece % half))
        return pl.multiple_of(target * cols + (step % per) * tile, tile)

    def copy_of(step, slot):
        return pltpu.make_async_copy(
            wd.at[0, :, pl.ds(start_col(step), tile)], buf.at[slot], sem.at[slot]
        )

    for step in range(slots):
        copy_of(step, step).start()

    each = share // 128

    def load_pair(pair):
        lane = pl.multiple_of((pair % each) * 128, 128)
        return arrived[pair // each, :, pl.ds(lane, 128)].astype(F32)

    for pair in range(hid // 128):
        mine[:, pl.ds(pair * 128, 128)] = place(
            load_pair, take_ref[2 * pair], take_ref[2 * pair + 1]
        )
    mask_all = mask_ref[...].astype(F32).astype(BF)

    def product(step):
        slot = lax.rem(step, slots)
        spread = (
            lax.broadcasted_iota(jnp.int32, (out_blocks, tile), 0)
            == (start_col(step) + lax.broadcasted_iota(jnp.int32, (out_blocks, tile), 1)) // width
        ).astype(BF)
        mask = jnp.dot(mask_all, spread, preferred_element_type=F32).astype(BF)
        copy_of(step, slot).wait()
        weight = (buf[slot].reshape(blocks, width, tile) * mask[:, None, :]).reshape(hid, tile)
        result = jnp.dot(mine[...], weight, preferred_element_type=F32)

        @pl.when(step + slots < steps)
        def _():
            copy_of(step + slots, slot).start()

        return result

    def pass_body(step, carry):
        part = pl.multiple_of((step % per) * tile, tile)
        pass_ref[step // per, :, pl.ds(part, tile)] = product(step).astype(BF)
        return carry

    def keep_body(step, carry):
        part = pl.multiple_of((step % per) * tile, tile)
        keep_ref[step // per - half, :, pl.ds(part, tile)] = product(step)
        return carry

    lax.fori_loop(0, steps // 2, pass_body, 0)
    lax.fori_loop(steps // 2, steps, keep_body, 0)
    keep_ref[0] += x_ref[...].astype(F32)


def down(me, take, arrived, x_own, mask, w_down):
    pieces, rows, share = arrived.shape
    hid, depth = w_down.shape[1:]
    tile, slots = 512, 4
    half = (pieces // 2, rows, depth // pieces)
    return pl.pallas_call(
        functools.partial(down_kernel, tile, slots),
        in_specs=[SM, SM, VM, VM, VM, HB],
        out_specs=(VM, VM),
        out_shape=(jax.ShapeDtypeStruct(half, F32), jax.ShapeDtypeStruct(half, BF)),
        scratch_shapes=[
            pltpu.VMEM((slots, hid, tile), BF),
            pltpu.SemaphoreType.DMA((slots,)),
            pltpu.VMEM((rows, hid), BF),
        ],
        compiler_params=pltpu.CompilerParams(vmem_limit_bytes=32 * MIB),
        cost_estimate=pl.CostEstimate(
            flops=2 * rows * depth * hid, bytes_accessed=2 * depth * hid, transcendentals=0
        ),
        name="down",
    )(me, take, arrived, x_own, mask, w_down)


def partner(block, distance):
    devices = range(lax.axis_size("tp"))
    return lax.ppermute(block, "tp", [(i, i ^ distance) for i in devices])


def onward(block, distance):
    tp_count = lax.axis_size("tp")
    sections = lax.axis_size("section")
    route = [
        (s * tp_count + t, (s + 1) % sections * tp_count + (t ^ distance))
        for s in range(sections)
        for t in range(tp_count)
    ]
    return lax.ppermute(block, ("section", "tp"), route)


def gathered(own):
    chips = lax.axis_size("tp") // 2
    near = jnp.stack([own] + [partner(own, 2 * k) for k in range(1, chips)])
    return jnp.concatenate([near, partner(near, 1)])


def exchanged(blocks):
    chips = blocks.shape[0] // 2
    share = blocks.shape[2]
    both = jnp.concatenate([blocks[:chips], partner(blocks[chips:], 1)], axis=2)
    got = jnp.stack([both[0]] + [partner(both[k], 2 * k) for k in range(1, chips)])
    return jnp.concatenate([got[:, :, :share], got[:, :, share:]])


def body(
    tokens,
    norm_gain,
    gate_weight,
    up_weight,
    gate_mask,
    up_mask,
    down_weight,
    down_mask,
    slot_order,
):
    sections = lax.axis_size("section")
    tp_count = lax.axis_size("tp")
    section_pos = lax.axis_index("section")
    tp_pos = lax.axis_index("tp")
    my_blocks = slot_order[0]
    per_device = my_blocks.shape[0]
    chips = tp_count // 2
    capacity = per_device // tp_count
    me = tp_pos.astype(jnp.int32).reshape(1)

    places = jnp.arange(tp_count, dtype=jnp.int32)
    away = places // chips + 2 * (places % chips)
    lanes = jnp.arange(per_device, dtype=jnp.int32)
    orders = lax.all_gather(my_blocks, "tp", axis=0)
    mine_there = orders // per_device == tp_pos
    ahead = lanes[None, :] < lanes[:, None]
    rank_there = jnp.sum(
        (mine_there[:, None, :] & ahead[None]).astype(jnp.int32), axis=2
    )
    ranks = jnp.arange(capacity, dtype=jnp.int32)
    picked = mine_there[:, None, :] & (rank_there[:, None, :] == ranks[None, :, None])
    to_send = jnp.sum(jnp.where(picked, orders[:, None, :] % per_device, 0), axis=2)
    at_place = (tp_pos ^ away)[:, None] == places[None, :]
    send = jnp.sum(jnp.where(at_place[:, :, None], to_send[None], 0), axis=1).reshape(-1)

    origin = my_blocks // per_device
    same = (origin[None, :] == origin[:, None]) & ahead
    rank = jnp.sum(same.astype(jnp.int32), axis=1)
    apart = origin ^ tp_pos
    take = (apart % 2 * chips + apart // 2) * capacity + rank

    x = gathered(tokens)
    saved = jnp.zeros(tokens.shape, BF)
    for round_pos in range(sections):
        blocks = gate_up(
            me, send, x, norm_gain, gate_mask[0], up_mask[0], gate_weight, up_weight
        )
        arrived = exchanged(blocks)
        kept, passed = down(me, take, arrived, x[0], down_mask[0], down_weight)
        sums = (kept + partner(passed, 1).astype(F32)).astype(BF)
        parts = [onward(sums[k], 2 * k).astype(F32) for k in range(chips)]
        own = functools.reduce(jnp.add, parts).astype(BF)
        saved = jnp.where(section_pos == (round_pos + 1) % sections, own, saved)
        if round_pos + 1 < sections:
            x = gathered(own)
    return saved[None]


def solution(mesh):
    tp_count = mesh.shape["tp"]
    line_body = body if tp_count == 8 else ring_body
    return jax.shard_map(
        line_body,
        mesh=mesh,
        in_specs=(
            P(None, "tp"),
            P("section", None),
            P("section", None, "tp"),
            P("section", None, "tp"),
            P("section", None, "tp"),
            P("section", None, "tp"),
            P("section", "tp", None),
            P("section", "tp", None),
            P("section", "tp"),
        ),
        out_specs=P("section", None, "tp"),
        check_vma=False,
    )
```

```python
import functools

import jax
import jax.numpy as jnp
from jax import lax
from jax.experimental import pallas as pl
from jax.experimental.pallas import tpu as pltpu
from jax.sharding import PartitionSpec as P


def passed_along(block, axis, distance):
    devices = range(lax.axis_size(axis))
    route = [((i - distance) % len(devices), i) for i in devices]
    return lax.ppermute(block, axis, route)


def expand_mask(mask, width):
    return jnp.repeat(jnp.repeat(mask, width, axis=0), width, axis=1)


def masked(weight, mask, width):
    return weight * expand_mask(mask, width).astype(jnp.bfloat16)


def ring_body(
    tokens,
    norm_gain,
    gate_weight,
    up_weight,
    gate_mask,
    up_mask,
    down_weight,
    down_mask,
    slot_order,
):
    sections = lax.axis_size("section")
    tp_count = lax.axis_size("tp")
    section_pos = lax.axis_index("section")
    tp_pos = lax.axis_index("tp")
    width = gate_weight.shape[1] // gate_mask.shape[1]
    w_gate = masked(gate_weight[0], gate_mask[0], width)
    w_up = masked(up_weight[0], up_mask[0], width)
    w_down = masked(down_weight[0], down_mask[0], width)
    gain = norm_gain[0]
    my_blocks = slot_order[0]
    per_device = my_blocks.shape[0]
    row_count, own_cols = tokens.shape
    window = min(tp_count, per_device)
    capacity = per_device // window
    slot_ids = jnp.arange(capacity, dtype=jnp.int32)
    my_source = my_blocks // per_device
    my_offset = (my_source - tp_pos) % tp_count
    lanes = jnp.arange(per_device, dtype=jnp.int32)
    earlier = (my_source[None, :] == my_source[:, None]) & (lanes[None, :] < lanes[:, None])
    my_rank = jnp.sum(earlier.astype(jnp.int32), axis=1)
    send_lists = []
    for offset in range(window):
        if offset == 0:
            table_row = my_blocks
        else:
            table_row = passed_along(my_blocks, "tp", offset)
        row_source = table_row // per_device
        row_block = table_row % per_device
        from_me = (row_source == tp_pos).astype(jnp.int32)
        order_rank = jnp.cumsum(from_me) - 1
        picks = (from_me[None, :] == 1) & (order_rank[None, :] == slot_ids[:, None])
        send_lists.append(jnp.sum(jnp.where(picks, row_block[None, :], 0), axis=1))
    x_full = lax.all_gather(tokens, "tp", axis=1, tiled=True)
    saved = jnp.zeros((row_count, own_cols), jnp.bfloat16)
    for round_pos in range(sections):
        x_own = lax.dynamic_slice_in_dim(x_full, tp_pos * own_cols, own_cols, 1)
        widened = x_full.astype(jnp.float32)
        scale = lax.rsqrt(jnp.mean(widened * widened, axis=-1, keepdims=True) + 1e-05)
        normed = (widened * scale * gain).astype(jnp.bfloat16)
        gate = jnp.dot(normed, w_gate, preferred_element_type=jnp.float32)
        upper = jnp.dot(normed, w_up, preferred_element_type=jnp.float32)
        hidden = (jax.nn.silu(gate) * upper).astype(jnp.bfloat16)
        flat = (
            hidden.reshape(row_count, per_device, width)
            .transpose(1, 0, 2)
            .reshape(per_device, row_count * width)
        )
        arrivals = []
        for gather_offset in range(window):
            outgoing = flat[send_lists[gather_offset]]
            if gather_offset == 0:
                arrivals.append(outgoing)
            else:
                arrivals.append(passed_along(outgoing, "tp", tp_count - gather_offset))
        stacked = jnp.stack(arrivals)
        chosen = stacked[my_offset, my_rank]
        mine = (
            chosen.reshape(per_device, row_count, width)
            .transpose(1, 0, 2)
            .reshape(row_count, per_device * width)
        )
        partial_sum = jnp.dot(mine, w_down, preferred_element_type=jnp.float32)
        summed = lax.psum_scatter(partial_sum, "tp", scatter_dimension=1, tiled=True)
        y_own = (x_own.astype(jnp.float32) + summed).astype(jnp.bfloat16)
        got_own = passed_along(y_own, "section", 1)
        if round_pos + 1 < sections:
            x_full = lax.all_gather(got_own, "tp", axis=1, tiled=True)
        saved = jnp.where(section_pos == (round_pos + 1) % sections, got_own, saved)
    return saved[None]


BF = jnp.bfloat16
F32 = jnp.float32
VM = pl.BlockSpec(memory_space=pltpu.VMEM)
SM = pl.BlockSpec(memory_space=pltpu.SMEM)
HB = pl.BlockSpec(memory_space=pltpu.HBM)
MIB = 2**20


def place(load_pair, first, second):
    lanes = lax.broadcasted_iota(jnp.int32, (1, 128), 1)
    left = pltpu.roll(load_pair(first // 2), 64 * (first % 2), 1)
    right = pltpu.roll(load_pair(second // 2), 64 * (1 - second % 2), 1)
    return jnp.where(lanes < 64, left, right).astype(BF)


GU_TILE, DN_TILE = 512, 512
GU_SLOTS, DN_SLOTS = 3, 3
GU_SPLIT, DN_SPLIT = 512, 256
GU_PARTS = ((0, 4), (1, 2, 3), (5, 6, 7))
GU_HELD = (0, 2, 2)
DN_PARTS = ((5, 7), (1, 3), (4, 6, 0, 2))
DN_HELD = (2, 4, 3)
HELD_PARTS = {
    "gate_up": [part for part, n in zip(GU_PARTS, GU_HELD) if n],
    "down": [part for part, n in zip(DN_PARTS, DN_HELD) if n],
}


def chosen(options, nth):
    value = options[0]
    for i, option in enumerate(options[1:]):
        value = jnp.where(nth == i + 1, option, value)
    return value


def place_of(me, piece):
    return me ^ (piece // 4 + 2 * (piece % 4))


def gate_up_row(me, pieces, cols, tile):
    per = cols // GU_TILE
    row = place_of(me, chosen(pieces, tile // per)) * cols + (tile % per) * GU_TILE
    return pl.multiple_of(row, GU_TILE)


def down_col(me, pieces, cols, tile):
    per = cols // DN_TILE
    col = place_of(me, chosen(pieces, tile // per)) * cols + (tile % per) * DN_TILE
    return pl.multiple_of(col, DN_TILE)


def spread_of(start, blocks, columns, width):
    return (
        lax.broadcasted_iota(jnp.int32, (blocks, columns), 0)
        == (start + lax.broadcasted_iota(jnp.int32, (blocks, columns), 1)) // width
    ).astype(BF)


def masks_kernel(gm_ref, um_ref, dm_ref, gu_masks, dn_masks):
    hid = gu_masks.shape[2]
    width = hid // gm_ref.shape[0]
    spread = spread_of(0, gm_ref.shape[0], hid, width)
    for j, mask in enumerate((gm_ref, um_ref)):
        gu_masks[j] = lax.dot_general(
            mask[...].astype(F32).astype(BF),
            spread,
            (((0,), (0,)), ((), ())),
            preferred_element_type=F32,
        )
    mask = dm_ref[...].astype(F32).astype(BF)

    def spread_down(tile, carry):
        spread = spread_of(tile * DN_TILE, dm_ref.shape[1], DN_TILE, width)
        dn_masks[tile] = jnp.dot(mask, spread, preferred_element_type=F32)
        return carry

    lax.fori_loop(0, dn_masks.shape[0], spread_down, 0)


def spread_masks(gate_mask, up_mask, down_mask, hid, depth):
    return pl.pallas_call(
        masks_kernel,
        in_specs=[VM, VM, VM],
        out_specs=(VM, VM),
        out_shape=(
            jax.ShapeDtypeStruct((2, gate_mask.shape[1], hid), F32),
            jax.ShapeDtypeStruct((depth // DN_TILE, down_mask.shape[0], DN_TILE), F32),
        ),
        compiler_params=pltpu.CompilerParams(vmem_limit_bytes=4 * MIB),
        name="spread_masks",
    )(gate_mask, up_mask, down_mask)


def slots_kernel(me_ref, orders, send_ref, take_ref, found, count):
    me = me_ref[0]
    pieces, per_device = orders.shape
    capacity = per_device // pieces

    def send_body(slot, ranks):
        after = []
        for piece, rank in enumerate(ranks):
            block = orders[piece, slot]
            found[piece * (capacity + 1) + rank] = lax.rem(block, per_device)
            after.append(rank + (lax.div(block, per_device) == me).astype(jnp.int32))
        return tuple(after)

    lax.fori_loop(0, per_device, send_body, (jnp.int32(0),) * pieces)
    for piece in range(pieces):
        count[piece] = 0
        for rank in range(capacity):
            send_ref[piece * capacity + rank] = found[piece * (capacity + 1) + rank]

    def take_body(slot, carry):
        apart = lax.div(orders[0, slot], per_device) ^ me
        piece = lax.rem(apart, 2) * (pieces // 2) + lax.div(apart, 2)
        rank = count[piece]
        take_ref[slot] = piece * capacity + rank
        count[piece] = rank + 1
        return carry

    lax.fori_loop(0, per_device, take_body, 0)


def slots(me, orders):
    pieces, per_device = orders.shape
    table = jax.ShapeDtypeStruct((per_device,), jnp.int32)
    return pl.pallas_call(
        slots_kernel,
        in_specs=[SM, SM],
        out_specs=(SM, SM),
        out_shape=(table, table),
        scratch_shapes=[
            pltpu.SMEM((per_device + pieces,), jnp.int32),
            pltpu.SMEM((pieces,), jnp.int32),
        ],
        compiler_params=pltpu.CompilerParams(vmem_limit_bytes=MIB),
        name="slots",
    )(me, orders)


def hold_kernel(which, me_ref, *refs):
    me = me_ref[0]
    if which == "gate_up":
        weights, held_refs, sem = refs[:2], refs[2:-1], refs[-1]
        cols = weights[0].shape[1] // 8
    else:
        weights, held_refs, sem = refs[:1], refs[1:-1], refs[-1]
        cols = weights[0].shape[2] // 8
    pairs = []
    for pieces, ref in zip(HELD_PARTS[which], held_refs):
        for tile in range(ref.shape[0]):
            if which == "gate_up":
                row = gate_up_row(me, pieces, cols, tile)
                for j, w in enumerate(weights):
                    pairs.append((w.at[0, pl.ds(row, GU_TILE)], ref.at[tile, j]))
            else:
                col = down_col(me, pieces, cols, tile)
                pairs.append((weights[0].at[0, :, pl.ds(col, DN_TILE)], ref.at[tile]))
    copies = [pltpu.make_async_copy(src, dst, sem.at[n]) for n, (src, dst) in enumerate(pairs)]
    for copy in copies:
        copy.start()
    for copy in copies:
        copy.wait()


def hold(which, me, weights):
    hid = weights[0].shape[2] if which == "gate_up" else weights[0].shape[1]
    if which == "gate_up":
        shapes = [jax.ShapeDtypeStruct((n, 2, GU_TILE, hid), BF) for n in GU_HELD if n]
        copies = 2 * sum(GU_HELD)
    else:
        shapes = [jax.ShapeDtypeStruct((n, hid, DN_TILE), BF) for n in DN_HELD if n]
        copies = sum(DN_HELD)
    moved = sum(2 * x.size for x in shapes)
    return pl.pallas_call(
        functools.partial(hold_kernel, which),
        in_specs=[SM] + [HB] * len(weights),
        out_specs=(VM,) * len(shapes),
        out_shape=tuple(shapes),
        scratch_shapes=[pltpu.SemaphoreType.DMA((copies,))],
        compiler_params=pltpu.CompilerParams(vmem_limit_bytes=2 * MIB),
        cost_estimate=pl.CostEstimate(flops=0, bytes_accessed=moved, transcendentals=0),
        name="hold",
    )(me, *weights)


def gate_up_kernel(part, n_x, n_before, n_held, me_ref, send_ref, gain_ref, masks, *refs):
    pieces = GU_PARTS[part]
    last = part == len(GU_PARTS) - 1
    x_refs, refs = refs[:n_x], refs[n_x:]
    before, refs = refs[: 2 * n_before], refs[2 * n_before :]
    if n_held:
        held, refs = refs[0], refs[1:]
    wg, wu = refs[:2]
    if last:
        out_ref, buf, sem, scaled, acc = refs[2:]
    else:
        acc, sq_ref, buf, sem, scaled = refs[2:]
    rows, cols = scaled.shape[1:]
    depth, hid = wg.shape[1:]
    width = depth // masks.shape[1]
    per = cols // GU_TILE
    kept = GU_TILE // width
    streamed = len(pieces) * per - n_held
    me = me_ref[0]

    def copies(nth, slot):
        row = gate_up_row(me, pieces, cols, n_held + nth)
        return [
            pltpu.make_async_copy(
                w.at[0, pl.ds(row, GU_TILE)], buf.at[slot, j], sem.at[slot, j]
            )
            for j, w in enumerate((wg, wu))
        ]

    for nth in range(GU_SLOTS):
        for copy in copies(nth, nth):
            copy.start()
    squares = jnp.zeros((rows, 128), F32)
    at = 0
    for x_ref in x_refs:
        for i in range(x_ref.shape[0]):
            start = pl.multiple_of(place_of(me, pieces[at]) * cols, cols)
            wide = x_ref[i, :, pl.ds(0, cols)].astype(F32)
            for lane in range(0, cols, 128):
                squares = squares + wide[:, lane : lane + 128] * wide[:, lane : lane + 128]
            scaled[at] = (wide * gain_ref[:, pl.ds(start, cols)]).astype(BF)
            at += 1
    if n_before:
        for j in range(2):
            total = before[0][j]
            for i in range(1, n_before):
                total = total + before[2 * i][j]
            acc[j] = total
        for i in range(n_before):
            squares = squares + before[2 * i + 1][...]
    else:
        acc[...] = jnp.zeros_like(acc)

    def add_product(tile, j, weight_ref):
        lanes = pl.ds(pl.multiple_of((tile % per) * GU_TILE, GU_TILE), GU_TILE)
        x_part = scaled[tile // per, :, lanes]
        row = gate_up_row(me, pieces, cols, tile)
        mask = masks[j, pl.ds(pl.multiple_of(row // width, kept), kept), :].astype(BF)
        for start in range(0, hid, GU_SPLIT):
            split = slice(start, start + GU_SPLIT)
            weight = weight_ref[:, split].reshape(kept, width, GU_SPLIT) * mask[:, None, split]
            acc[j, :, split] += jnp.dot(
                x_part, weight.reshape(GU_TILE, GU_SPLIT), preferred_element_type=F32
            )

    def step_body(with_held, nth, carry):
        slot = lax.rem(nth, GU_SLOTS)
        for j, copy in enumerate(copies(nth, slot)):
            if with_held:
                add_product(nth, j, held.at[nth, j])
            copy.wait()
            add_product(n_held + nth, j, buf.at[slot, j])

        @pl.when(nth + GU_SLOTS < streamed)
        def _():
            for copy in copies(nth + GU_SLOTS, slot):
                copy.start()

        return carry

    assert n_held <= streamed
    if n_held:
        lax.fori_loop(0, n_held, functools.partial(step_body, True), 0)
    if n_held < streamed:
        lax.fori_loop(n_held, streamed, functools.partial(step_body, False), 0)
    if not last:
        sq_ref[...] = squares
        return
    scale = lax.rsqrt(jnp.sum(squares, axis=1, keepdims=True) / depth + 1e-05)
    gate = acc[0] * scale
    hidden = (gate / (1.0 + jnp.exp(-gate)) * (acc[1] * scale)).astype(BF)
    acc[0] = hidden.astype(F32)

    def load_pair(pair):
        return acc[0, :, pl.ds(pl.multiple_of(pair * 128, 128), 128)]

    each = out_ref.shape[2] // 128
    for piece in range(out_ref.shape[0]):
        for pair in range(each):
            at = piece * 2 * each + 2 * pair
            out_ref[piece, :, pl.ds(pair * 128, 128)] = place(
                load_pair, send_ref[at], send_ref[at + 1]
            )


def gate_up(part, me, send, gain, masks, xs, before, held, w_gate, w_up):
    rows = xs[0].shape[1]
    depth, hid = w_gate.shape[1:]
    cols = depth // 8
    pieces = len(GU_PARTS[part])
    last = part == len(GU_PARTS) - 1
    acc = (2, rows, hid)
    scratch = [
        pltpu.VMEM((GU_SLOTS, 2, GU_TILE, hid), BF),
        pltpu.SemaphoreType.DMA((GU_SLOTS, 2)),
        pltpu.VMEM((pieces, rows, cols), BF),
    ]
    if last:
        out_specs, out_shape = VM, jax.ShapeDtypeStruct((8, rows, hid // 8), BF)
        scratch.append(pltpu.VMEM(acc, F32))
    else:
        out_specs = (VM, VM)
        out_shape = (jax.ShapeDtypeStruct(acc, F32), jax.ShapeDtypeStruct((rows, 128), F32))
    operands = list(xs) + list(before) + list(held)
    n_held = held[0].shape[0] if held else 0
    return pl.pallas_call(
        functools.partial(gate_up_kernel, part, len(xs), len(before) // 2, n_held),
        in_specs=[SM, SM, VM, VM] + [VM] * len(operands) + [HB, HB],
        out_specs=out_specs,
        out_shape=out_shape,
        scratch_shapes=scratch,
        compiler_params=pltpu.CompilerParams(vmem_limit_bytes=15 * MIB),
        cost_estimate=pl.CostEstimate(
            flops=4 * rows * pieces * cols * hid,
            bytes_accessed=4 * (pieces * cols - n_held * GU_TILE) * hid,
            transcendentals=0,
        ),
        name="gate_up",
    )(me, send, gain, masks, *operands, w_gate, w_up)


def down_kernel(part, n_held, me_ref, take_ref, inner_ref, x_ref, masks, *refs):
    pieces = DN_PARTS[part]
    if n_held:
        held, refs = refs[0], refs[1:]
    wd, refs = refs[0], refs[1:]
    first, last = part == 0, part == len(DN_PARTS) - 1
    if first:
        out_ref, mine, buf, sem = refs
    elif last:
        out_ref, pass_ref, buf, sem = refs
    else:
        out_ref, buf, sem = refs
    if not first:
        mine = inner_ref
    hid, depth = wd.shape[1:]
    cols = depth // 8
    blocks = masks.shape[1]
    width = hid // blocks
    per = cols // DN_TILE
    streamed = len(pieces) * per - n_held
    n_slots = min(DN_SLOTS, streamed)
    me = me_ref[0]

    def copy_of(nth, slot):
        col = down_col(me, pieces, cols, n_held + nth)
        return pltpu.make_async_copy(wd.at[0, :, pl.ds(col, DN_TILE)], buf.at[slot], sem.at[slot])

    for nth in range(n_slots):
        copy_of(nth, nth).start()
    if first:
        each = inner_ref.shape[2] // 128

        def load_pair(pair):
            lane = pl.multiple_of((pair % each) * 128, 128)
            return inner_ref[pair // each, :, pl.ds(lane, 128)].astype(F32)

        for pair in range(hid // 128):
            mine[:, pl.ds(pair * 128, 128)] = place(
                load_pair, take_ref[2 * pair], take_ref[2 * pair + 1]
            )

    def put(tile, weight_ref):
        mask = masks[down_col(me, pieces, cols, tile) // DN_TILE].astype(BF)
        for start in range(0, DN_TILE, DN_SPLIT):
            split = slice(start, start + DN_SPLIT)
            weight = weight_ref[:, split].reshape(blocks, width, DN_SPLIT) * mask[:, None, split]
            result = jnp.dot(
                mine[...], weight.reshape(hid, DN_SPLIT), preferred_element_type=F32
            )
            lanes = pl.ds(pl.multiple_of((tile % per) * DN_TILE + start, DN_SPLIT), DN_SPLIT)
            out_ref[tile // per, :, lanes] = result.astype(out_ref.dtype)

    def held_body(nth, carry):
        put(nth, held.at[nth])
        return carry

    def step_body(with_held, nth, carry):
        slot = lax.rem(nth, n_slots)
        if with_held:
            put(nth, held.at[nth])
        copy_of(nth, slot).wait()
        put(n_held + nth, buf.at[slot])

        @pl.when(nth + n_slots < streamed)
        def _():
            copy_of(nth + n_slots, slot).start()

        return carry

    both = min(n_held, streamed)
    if both < n_held:
        lax.fori_loop(both, n_held, held_body, 0)
    if both:
        lax.fori_loop(0, both, functools.partial(step_body, True), 0)
    if both < streamed:
        lax.fori_loop(both, streamed, functools.partial(step_body, False), 0)
    if last:
        passed = pass_ref.shape[0]
        pass_ref[...] = out_ref[pl.ds(0, passed)].astype(BF)
        out_ref[passed] += x_ref[:, pl.ds(0, cols)].astype(F32)


def down(part, me, take, inner, x_own, masks, held, w_down):
    hid, depth = w_down.shape[1:]
    rows = x_own.shape[0]
    cols = depth // 8
    pieces = len(DN_PARTS[part])
    n_held = held[0].shape[0] if held else 0
    out = [jax.ShapeDtypeStruct((pieces, rows, cols), F32 if part else BF)]
    if part == 0:
        out.append(jax.ShapeDtypeStruct((rows, hid), BF))
    if part == len(DN_PARTS) - 1:
        out.append(jax.ShapeDtypeStruct((pieces // 2, rows, cols), BF))
    return pl.pallas_call(
        functools.partial(down_kernel, part, n_held),
        in_specs=[SM, SM, VM, VM, VM] + [VM] * len(held) + [HB],
        out_specs=(VM,) * len(out),
        out_shape=tuple(out),
        scratch_shapes=[
            pltpu.VMEM((DN_SLOTS, hid, DN_TILE), BF),
            pltpu.SemaphoreType.DMA((DN_SLOTS,)),
        ],
        compiler_params=pltpu.CompilerParams(vmem_limit_bytes=9 * MIB),
        cost_estimate=pl.CostEstimate(
            flops=2 * rows * pieces * cols * hid,
            bytes_accessed=2 * (pieces * cols - n_held * DN_TILE) * hid,
            transcendentals=0,
        ),
        name="down",
    )(me, take, inner, x_own, masks, *held, w_down)


def partner(block, distance):
    devices = range(lax.axis_size("tp"))
    return lax.ppermute(block, "tp", [(i, i ^ distance) for i in devices])


def onward(block, distance):
    tp_count = lax.axis_size("tp")
    sections = lax.axis_size("section")
    route = [
        (s * tp_count + t, (s + 1) % sections * tp_count + (t ^ distance))
        for s in range(sections)
        for t in range(tp_count)
    ]
    return lax.ppermute(block, ("section", "tp"), route)


def beside_exchanged(blocks):
    chips = blocks.shape[0] // 2
    return jnp.concatenate([blocks[:chips], partner(blocks[chips:], 1)], axis=2)


def along_exchanged(both):
    return [both[0]] + [partner(both[k], 2 * k) for k in range(1, both.shape[0])]


def sorted_arrivals(got):
    got = jnp.stack(got)
    share = got.shape[2] // 2
    return jnp.concatenate([got[:, :, :share], got[:, :, share:]])


def line_of_eight(
    tokens,
    norm_gain,
    gate_weight,
    up_weight,
    gate_mask,
    up_mask,
    down_weight,
    down_mask,
    slot_order,
):
    sections = lax.axis_size("section")
    tp_count = lax.axis_size("tp")
    section_pos = lax.axis_index("section")
    tp_pos = lax.axis_index("tp")
    rows, cols = tokens.shape
    my_blocks = slot_order[0]
    per_device = my_blocks.shape[0]
    chips = tp_count // 2
    me = tp_pos.astype(jnp.int32).reshape(1)

    gate_weight, up_weight, down_weight = (
        pltpu.with_memory_space_constraint(w, pltpu.HBM)
        for w in (gate_weight, up_weight, down_weight)
    )
    numbers = jnp.pad(my_blocks, (0, 128 - per_device)).astype(BF)
    own = jnp.concatenate([tokens, jnp.broadcast_to(numbers[None], (rows, 128))], axis=1)
    send = jnp.zeros((per_device,), jnp.int32)
    gu_masks, dn_masks = spread_masks(
        gate_mask[0].T, up_mask[0].T, down_mask[0], gate_weight.shape[2], down_weight.shape[2]
    )
    gu_held = [[]] * len(GU_HELD)
    saved = jnp.zeros(tokens.shape, BF)
    for round_pos in range(sections):
        straight = [partner(own, 2 * k) for k in range(1, chips)]
        beside = partner(own, 1)
        arrivals = gate_up(
            0, me, send, norm_gain, gu_masks, [own[None], beside[None]], [], gu_held[0],
            gate_weight, up_weight,
        )
        straight, arrivals = lax.optimization_barrier((straight, arrivals))
        near = jnp.stack(straight)
        far = partner(near, 1)
        arrivals = gate_up(
            1, me, send, norm_gain, gu_masks, [near], arrivals, gu_held[1],
            gate_weight, up_weight,
        )
        far, arrivals = lax.optimization_barrier((far, arrivals))
        if round_pos == 0:
            there = [own[None], near, beside[None], far]
            orders = jnp.concatenate([x[:, 0, cols : cols + per_device] for x in there])
            send, take = slots(me, orders.astype(jnp.int32))
        blocks = gate_up(
            2, me, send, norm_gain, gu_masks, [far], arrivals, gu_held[2],
            gate_weight, up_weight,
        )
        both = beside_exchanged(blocks)
        if round_pos == 0:
            both, turn = lax.optimization_barrier((both, me))
            kept_tiles = hold("down", turn, (down_weight,))
        got = along_exchanged(both)
        if round_pos == 0:
            got, kept_tiles = lax.optimization_barrier((got, kept_tiles))
            kept_tiles = list(kept_tiles)
            dn_held = [[kept_tiles.pop(0)] if count else [] for count in DN_HELD]
        arrived = sorted_arrivals(got)
        passed, mine = down(0, me, take, arrived, own, dn_masks, dn_held[0], down_weight)
        got = partner(passed, 1).astype(F32)
        (kept,) = down(1, me, take, mine, own, dn_masks, dn_held[1], down_weight)
        outward, mine = lax.optimization_barrier(((kept + got).astype(BF), mine))
        nearer = partner(outward, 2)
        kept, passed = down(2, me, take, mine, own, dn_masks, dn_held[2], down_weight)
        nearer, kept, passed = lax.optimization_barrier((nearer, kept, passed))
        sums = kept[2:] + partner(passed, 1).astype(F32) + nearer.astype(F32)
        sums = sums.astype(BF)
        if round_pos == 0:
            sums, turn = lax.optimization_barrier((sums, me))
            kept_tiles = hold("gate_up", turn, (gate_weight, up_weight))
        halves = [onward(sums[0], 0), onward(sums[1], 4)]
        if round_pos == 0:
            halves, kept_tiles = lax.optimization_barrier((halves, kept_tiles))
            kept_tiles = list(kept_tiles)
            gu_held = [[kept_tiles.pop(0)] if count else [] for count in GU_HELD]
        own = (halves[0].astype(F32) + halves[1].astype(F32)).astype(BF)
        saved = jnp.where(section_pos == (round_pos + 1) % sections, own, saved)
    return saved[None]


def solution(mesh):
    tp_count = mesh.shape["tp"]
    line_body = line_of_eight if tp_count == 8 else ring_body
    return jax.shard_map(
        line_body,
        mesh=mesh,
        in_specs=(
            P(None, "tp"),
            P("section", None),
            P("section", None, "tp"),
            P("section", None, "tp"),
            P("section", None, "tp"),
            P("section", None, "tp"),
            P("section", "tp", None),
            P("section", "tp", None),
            P("section", "tp"),
        ),
        out_specs=P("section", None, "tp"),
        check_vma=False,
    )
```

```python
import functools

import jax
import jax.numpy as jnp
from jax import lax
from jax.experimental import pallas as pl
from jax.experimental.pallas import tpu as pltpu
from jax.sharding import PartitionSpec as P


def passed_along(block, axis, distance):
    devices = range(lax.axis_size(axis))
    route = [((i - distance) % len(devices), i) for i in devices]
    return lax.ppermute(block, axis, route)


def expand_mask(mask, width):
    return jnp.repeat(jnp.repeat(mask, width, axis=0), width, axis=1)


def masked(weight, mask, width):
    return weight * expand_mask(mask, width).astype(jnp.bfloat16)


def ring_body(
    tokens,
    norm_gain,
    gate_weight,
    up_weight,
    gate_mask,
    up_mask,
    down_weight,
    down_mask,
    slot_order,
):
    sections = lax.axis_size("section")
    tp_count = lax.axis_size("tp")
    section_pos = lax.axis_index("section")
    tp_pos = lax.axis_index("tp")
    width = gate_weight.shape[1] // gate_mask.shape[1]
    w_gate = masked(gate_weight[0], gate_mask[0], width)
    w_up = masked(up_weight[0], up_mask[0], width)
    w_down = masked(down_weight[0], down_mask[0], width)
    gain = norm_gain[0]
    my_blocks = slot_order[0]
    per_device = my_blocks.shape[0]
    row_count, own_cols = tokens.shape
    window = min(tp_count, per_device)
    capacity = per_device // window
    slot_ids = jnp.arange(capacity, dtype=jnp.int32)
    my_source = my_blocks // per_device
    my_offset = (my_source - tp_pos) % tp_count
    lanes = jnp.arange(per_device, dtype=jnp.int32)
    earlier = (my_source[None, :] == my_source[:, None]) & (lanes[None, :] < lanes[:, None])
    my_rank = jnp.sum(earlier.astype(jnp.int32), axis=1)
    send_lists = []
    for offset in range(window):
        if offset == 0:
            table_row = my_blocks
        else:
            table_row = passed_along(my_blocks, "tp", offset)
        row_source = table_row // per_device
        row_block = table_row % per_device
        from_me = (row_source == tp_pos).astype(jnp.int32)
        order_rank = jnp.cumsum(from_me) - 1
        picks = (from_me[None, :] == 1) & (order_rank[None, :] == slot_ids[:, None])
        send_lists.append(jnp.sum(jnp.where(picks, row_block[None, :], 0), axis=1))
    x_full = lax.all_gather(tokens, "tp", axis=1, tiled=True)
    saved = jnp.zeros((row_count, own_cols), jnp.bfloat16)
    for round_pos in range(sections):
        x_own = lax.dynamic_slice_in_dim(x_full, tp_pos * own_cols, own_cols, 1)
        widened = x_full.astype(jnp.float32)
        scale = lax.rsqrt(jnp.mean(widened * widened, axis=-1, keepdims=True) + 1e-05)
        normed = (widened * scale * gain).astype(jnp.bfloat16)
        gate = jnp.dot(normed, w_gate, preferred_element_type=jnp.float32)
        upper = jnp.dot(normed, w_up, preferred_element_type=jnp.float32)
        hidden = (jax.nn.silu(gate) * upper).astype(jnp.bfloat16)
        flat = (
            hidden.reshape(row_count, per_device, width)
            .transpose(1, 0, 2)
            .reshape(per_device, row_count * width)
        )
        arrivals = []
        for gather_offset in range(window):
            outgoing = flat[send_lists[gather_offset]]
            if gather_offset == 0:
                arrivals.append(outgoing)
            else:
                arrivals.append(passed_along(outgoing, "tp", tp_count - gather_offset))
        stacked = jnp.stack(arrivals)
        chosen = stacked[my_offset, my_rank]
        mine = (
            chosen.reshape(per_device, row_count, width)
            .transpose(1, 0, 2)
            .reshape(row_count, per_device * width)
        )
        partial_sum = jnp.dot(mine, w_down, preferred_element_type=jnp.float32)
        summed = lax.psum_scatter(partial_sum, "tp", scatter_dimension=1, tiled=True)
        y_own = (x_own.astype(jnp.float32) + summed).astype(jnp.bfloat16)
        got_own = passed_along(y_own, "section", 1)
        if round_pos + 1 < sections:
            x_full = lax.all_gather(got_own, "tp", axis=1, tiled=True)
        saved = jnp.where(section_pos == (round_pos + 1) % sections, got_own, saved)
    return saved[None]


BF = jnp.bfloat16
F32 = jnp.float32
VM = pl.BlockSpec(memory_space=pltpu.VMEM)
SM = pl.BlockSpec(memory_space=pltpu.SMEM)
HB = pl.BlockSpec(memory_space=pltpu.HBM)
MIB = 2**20


def place(load_pair, first, second):
    lanes = lax.broadcasted_iota(jnp.int32, (1, 128), 1)
    left = pltpu.roll(load_pair(first // 2), 64 * (first % 2), 1)
    right = pltpu.roll(load_pair(second // 2), 64 * (1 - second % 2), 1)
    return jnp.where(lanes < 64, left, right).astype(BF)


GU_TILE, DN_TILE = 512, 512
GU_SLOTS, DN_SLOTS = 3, 3
GU_SPLIT, DN_SPLIT = 512, 256
GU_PARTS = ((0, 4), (3,), (2, 1), (7, 6, 5), (3, 2, 1))
GU_HELD = (0, 1, 2, 4, 0)
DN_PARTS = ((5, 7), (1, 3), (4, 6, 0, 2))
DN_HELD = (3, 4, 3)
GU_LAST, GU_FIRST_ROUND = 3, 4
GU_BROUGHT, GU_STAYING = (1, 2), (3,)


def chosen(options, nth):
    value = options[0]
    for i, option in enumerate(options[1:]):
        value = jnp.where(nth == i + 1, option, value)
    return value


def place_of(me, piece):
    return me ^ (piece // 4 + 2 * (piece % 4))


def gate_up_row(me, pieces, cols, tile):
    per = cols // GU_TILE
    row = place_of(me, chosen(pieces, tile // per)) * cols + (tile % per) * GU_TILE
    return pl.multiple_of(row, GU_TILE)


def down_col(me, pieces, cols, tile):
    per = cols // DN_TILE
    col = place_of(me, chosen(pieces, tile // per)) * cols + (tile % per) * DN_TILE
    return pl.multiple_of(col, DN_TILE)


def spread_of(start, blocks, columns, width):
    return (
        lax.broadcasted_iota(jnp.int32, (blocks, columns), 0)
        == (start + lax.broadcasted_iota(jnp.int32, (blocks, columns), 1)) // width
    ).astype(BF)


def masks_kernel(gm, um, dm, gain, gu_masks, dn_masks, gain_ref, gm_ref, um_ref, dm_ref, sem):
    pairs = ((gm, gm_ref), (um, um_ref), (dm, dm_ref), (gain, gain_ref))
    copies = [pltpu.make_async_copy(src, dst, sem.at[n]) for n, (src, dst) in enumerate(pairs)]
    for copy in copies:
        copy.start()
    hid = gu_masks.shape[2]
    blocks = gm_ref.shape[0]
    spread = spread_of(0, blocks, hid, hid // blocks)
    for copy in copies:
        copy.wait()
    for j, mask in enumerate((gm_ref, um_ref)):
        gu_masks[j] = lax.dot_general(
            mask[...].astype(F32).astype(BF),
            spread,
            (((0,), (0,)), ((), ())),
            preferred_element_type=F32,
        )
    per = hid // DN_TILE
    for start in range(0, dm_ref.shape[1], blocks):
        mask = dm_ref[:, start : start + blocks].astype(F32).astype(BF)
        wide = jnp.dot(mask, spread, preferred_element_type=F32)
        for i in range(per):
            dn_masks[start // blocks * per + i] = wide[:, i * DN_TILE : (i + 1) * DN_TILE]


def spread_masks(gate_mask, up_mask, down_mask, gain, hid, depth):
    operands = [
        pltpu.with_memory_space_constraint(x, pltpu.HBM)
        for x in (gate_mask, up_mask, down_mask, gain)
    ]
    return pl.pallas_call(
        masks_kernel,
        in_specs=[HB] * 4,
        out_specs=(VM, VM, VM),
        out_shape=(
            jax.ShapeDtypeStruct((2, gate_mask.shape[1], hid), F32),
            jax.ShapeDtypeStruct((depth // DN_TILE, down_mask.shape[0], DN_TILE), F32),
            jax.ShapeDtypeStruct(gain.shape, F32),
        ),
        scratch_shapes=[pltpu.VMEM(x.shape, jnp.int32) for x in operands[:3]]
        + [pltpu.SemaphoreType.DMA((4,))],
        compiler_params=pltpu.CompilerParams(vmem_limit_bytes=4 * MIB),
        name="spread_masks",
    )(*operands)


def slots_kernel(cols, per_device, order, me_ref, *refs):
    x_refs, refs = refs[: len(order)], refs[len(order) :]
    send_ref, take_ref, table, orders, sem, found, count = refs
    me = me_ref[0]
    for x_ref, places in zip(x_refs, order):
        for i, piece in enumerate(places):
            row = x_ref[i, pl.ds(0, 16), pl.ds(cols, 128)].astype(F32)[0:1]
            table[pl.ds(piece, 1), :] = row.astype(jnp.int32)
    copy = pltpu.make_async_copy(table, orders, sem)
    copy.start()
    copy.wait()
    pieces = orders.shape[0]
    capacity = per_device // pieces

    def send_body(slot, ranks):
        after = []
        for piece, rank in enumerate(ranks):
            block = orders[piece, slot]
            found[piece * (capacity + 1) + rank] = lax.rem(block, per_device)
            after.append(rank + (lax.div(block, per_device) == me).astype(jnp.int32))
        return tuple(after)

    lax.fori_loop(0, per_device, send_body, (jnp.int32(0),) * pieces)
    for piece in range(pieces):
        count[piece] = 0
        for rank in range(capacity):
            send_ref[piece * capacity + rank] = found[piece * (capacity + 1) + rank]

    def take_body(slot, carry):
        apart = lax.div(orders[0, slot], per_device) ^ me
        piece = lax.rem(apart, 2) * (pieces // 2) + lax.div(apart, 2)
        rank = count[piece]
        take_ref[slot] = piece * capacity + rank
        count[piece] = rank + 1
        return carry

    lax.fori_loop(0, per_device, take_body, 0)


def slots(me, xs, order, cols, per_device):
    pieces = sum(len(places) for places in order)
    table = jax.ShapeDtypeStruct((per_device,), jnp.int32)
    return pl.pallas_call(
        functools.partial(slots_kernel, cols, per_device, order),
        in_specs=[SM] + [VM] * len(xs),
        out_specs=(SM, SM),
        out_shape=(table, table),
        scratch_shapes=[
            pltpu.VMEM((pieces, 128), jnp.int32),
            pltpu.SMEM((pieces, 128), jnp.int32),
            pltpu.SemaphoreType.DMA,
            pltpu.SMEM((per_device + pieces,), jnp.int32),
            pltpu.SMEM((pieces,), jnp.int32),
        ],
        compiler_params=pltpu.CompilerParams(vmem_limit_bytes=MIB),
        name="slots",
    )(me, *xs)


def hold_kernel(parts, me_ref, *refs):
    me = me_ref[0]
    sem = refs[-1]
    weights, held_refs = refs[: -1 - len(parts)], refs[-1 - len(parts) : -1]
    pairs = []
    for pieces, ref in zip(parts, held_refs):
        for tile in range(ref.shape[0]):
            if len(weights) == 2:
                row = gate_up_row(me, pieces, weights[0].shape[1] // 8, tile)
                for j, w in enumerate(weights):
                    pairs.append((w.at[0, pl.ds(row, GU_TILE)], ref.at[tile, j]))
            else:
                col = down_col(me, pieces, weights[0].shape[2] // 8, tile)
                pairs.append((weights[0].at[0, :, pl.ds(col, DN_TILE)], ref.at[tile]))
    copies = [pltpu.make_async_copy(src, dst, sem.at[n]) for n, (src, dst) in enumerate(pairs)]
    for copy in copies:
        copy.start()
    for copy in copies:
        copy.wait()


def hold(parts, counts, me, weights):
    if len(weights) == 2:
        shapes = [(n, 2, GU_TILE, weights[0].shape[2]) for n in counts]
    else:
        shapes = [(n, weights[0].shape[1], DN_TILE) for n in counts]
    shapes = [jax.ShapeDtypeStruct(shape, BF) for shape in shapes]
    return pl.pallas_call(
        functools.partial(hold_kernel, parts),
        in_specs=[SM] + [HB] * len(weights),
        out_specs=(VM,) * len(shapes),
        out_shape=tuple(shapes),
        scratch_shapes=[pltpu.SemaphoreType.DMA((len(weights) * sum(counts),))],
        compiler_params=pltpu.CompilerParams(vmem_limit_bytes=2 * MIB),
        cost_estimate=pl.CostEstimate(
            flops=0, bytes_accessed=sum(2 * x.size for x in shapes), transcendentals=0
        ),
        name="hold",
    )(me, *weights)


def gate_up_kernel(part, n_x, n_before, n_held, me_ref, send_ref, gain_ref, masks, *refs):
    pieces = GU_PARTS[part]
    last = part == GU_LAST
    x_refs, refs = refs[:n_x], refs[n_x:]
    before, refs = refs[: 2 * n_before], refs[2 * n_before :]
    if n_held:
        held, refs = refs[0], refs[1:]
    wg, wu = refs[:2]
    if last:
        out_ref, buf, sem, scaled, acc = refs[2:]
    else:
        acc, sq_ref, buf, sem, scaled = refs[2:]
    rows, cols = scaled.shape[1:]
    depth, hid = wg.shape[1:]
    width = depth // masks.shape[1]
    per = cols // GU_TILE
    kept = GU_TILE // width
    streamed = len(pieces) * per - n_held
    me = me_ref[0]

    def copies(nth, slot):
        row = gate_up_row(me, pieces, cols, n_held + nth)
        return [
            pltpu.make_async_copy(
                w.at[0, pl.ds(row, GU_TILE)], buf.at[slot, j], sem.at[slot, j]
            )
            for j, w in enumerate((wg, wu))
        ]

    slots = min(GU_SLOTS, streamed)
    for nth in range(slots):
        for copy in copies(nth, nth):
            copy.start()
    squares = jnp.zeros((rows, 128), F32)
    at = 0
    for x_ref in x_refs:
        for i in range(x_ref.shape[0]):
            start = pl.multiple_of(place_of(me, pieces[at]) * cols, cols)
            wide = x_ref[i, :, pl.ds(0, cols)].astype(F32)
            for lane in range(0, cols, 128):
                squares = squares + wide[:, lane : lane + 128] * wide[:, lane : lane + 128]
            scaled[at] = (wide * gain_ref[:, pl.ds(start, cols)]).astype(BF)
            at += 1
    if n_before:
        for j in range(2):
            total = before[0][j]
            for i in range(1, n_before):
                total = total + before[2 * i][j]
            acc[j] = total
        for i in range(n_before):
            squares = squares + before[2 * i + 1][...]
    else:
        acc[...] = jnp.zeros_like(acc)

    def add_product(tile, j, weight_ref):
        lanes = pl.ds(pl.multiple_of((tile % per) * GU_TILE, GU_TILE), GU_TILE)
        x_part = scaled[tile // per, :, lanes]
        row = gate_up_row(me, pieces, cols, tile)
        mask = masks[j, pl.ds(pl.multiple_of(row // width, kept), kept), :].astype(BF)
        for start in range(0, hid, GU_SPLIT):
            split = slice(start, start + GU_SPLIT)
            weight = weight_ref[:, split].reshape(kept, width, GU_SPLIT) * mask[:, None, split]
            acc[j, :, split] += jnp.dot(
                x_part, weight.reshape(GU_TILE, GU_SPLIT), preferred_element_type=F32
            )

    def step_body(with_held, nth, carry):
        slot = lax.rem(nth, slots)
        for j, copy in enumerate(copies(nth, slot)):
            if with_held:
                add_product(nth, j, held.at[nth, j])
            copy.wait()
            add_product(n_held + nth, j, buf.at[slot, j])

        @pl.when(nth + slots < streamed)
        def _():
            for copy in copies(nth + slots, slot):
                copy.start()

        return carry

    def held_body(nth, carry):
        for j in range(2):
            add_product(nth, j, held.at[nth, j])
        return carry

    both = min(n_held, streamed)
    if both < n_held:
        lax.fori_loop(both, n_held, held_body, 0)
    if both:
        lax.fori_loop(0, both, functools.partial(step_body, True), 0)
    if both < streamed:
        lax.fori_loop(both, streamed, functools.partial(step_body, False), 0)
    if not last:
        sq_ref[...] = squares
        return
    scale = lax.rsqrt(jnp.sum(squares, axis=1, keepdims=True) / depth + 1e-05)
    gate = acc[0] * scale
    hidden = (gate / (1.0 + jnp.exp(-gate)) * (acc[1] * scale)).astype(BF)
    acc[0] = hidden.astype(F32)

    def load_pair(pair):
        return acc[0, :, pl.ds(pl.multiple_of(pair * 128, 128), 128)]

    each = out_ref.shape[2] // 128
    for piece in range(out_ref.shape[0]):
        for pair in range(each):
            at = piece * 2 * each + 2 * pair
            out_ref[piece, :, pl.ds(pair * 128, 128)] = place(
                load_pair, send_ref[at], send_ref[at + 1]
            )


def gate_up(part, me, send, gain, masks, xs, before, held, w_gate, w_up):
    rows = xs[0].shape[1]
    depth, hid = w_gate.shape[1:]
    cols = depth // 8
    pieces = len(GU_PARTS[part])
    last = part == GU_LAST
    acc = (2, rows, hid)
    scratch = [
        pltpu.VMEM((GU_SLOTS, 2, GU_TILE, hid), BF),
        pltpu.SemaphoreType.DMA((GU_SLOTS, 2)),
        pltpu.VMEM((pieces, rows, cols), BF),
    ]
    if last:
        out_specs, out_shape = VM, jax.ShapeDtypeStruct((8, rows, hid // 8), BF)
        scratch.append(pltpu.VMEM(acc, F32))
    else:
        out_specs = (VM, VM)
        out_shape = (jax.ShapeDtypeStruct(acc, F32), jax.ShapeDtypeStruct((rows, 128), F32))
    operands = list(xs) + list(before) + list(held)
    n_held = held[0].shape[0] if held else 0
    return pl.pallas_call(
        functools.partial(gate_up_kernel, part, len(xs), len(before) // 2, n_held),
        in_specs=[SM, SM, VM, VM] + [VM] * len(operands) + [HB, HB],
        out_specs=out_specs,
        out_shape=out_shape,
        scratch_shapes=scratch,
        compiler_params=pltpu.CompilerParams(vmem_limit_bytes=15 * MIB),
        cost_estimate=pl.CostEstimate(
            flops=4 * rows * pieces * cols * hid,
            bytes_accessed=4 * (pieces * cols - n_held * GU_TILE) * hid,
            transcendentals=0,
        ),
        name="gate_up",
    )(me, send, gain, masks, *operands, w_gate, w_up)


def down_kernel(part, n_held, me_ref, take_ref, inner_ref, x_ref, masks, *refs):
    pieces = DN_PARTS[part]
    if n_held:
        held, refs = refs[0], refs[1:]
    wd, refs = refs[0], refs[1:]
    first, last = part == 0, part == len(DN_PARTS) - 1
    if first:
        out_ref, mine, buf, sem = refs
    elif last:
        out_ref, pass_ref, buf, sem = refs
    else:
        out_ref, buf, sem = refs
    if not first:
        mine = inner_ref
    hid, depth = wd.shape[1:]
    cols = depth // 8
    blocks = masks.shape[1]
    width = hid // blocks
    per = cols // DN_TILE
    streamed = len(pieces) * per - n_held
    n_slots = min(DN_SLOTS, streamed)
    me = me_ref[0]

    def copy_of(nth, slot):
        col = down_col(me, pieces, cols, n_held + nth)
        return pltpu.make_async_copy(wd.at[0, :, pl.ds(col, DN_TILE)], buf.at[slot], sem.at[slot])

    for nth in range(n_slots):
        copy_of(nth, nth).start()
    if first:
        each = inner_ref.shape[2] // 128

        def load_pair(pair):
            lane = pl.multiple_of((pair % each) * 128, 128)
            return inner_ref[pair // each, :, pl.ds(lane, 128)].astype(F32)

        for pair in range(hid // 128):
            mine[:, pl.ds(pair * 128, 128)] = place(
                load_pair, take_ref[2 * pair], take_ref[2 * pair + 1]
            )

    def put(tile, weight_ref):
        mask = masks[down_col(me, pieces, cols, tile) // DN_TILE].astype(BF)
        for start in range(0, DN_TILE, DN_SPLIT):
            split = slice(start, start + DN_SPLIT)
            weight = weight_ref[:, split].reshape(blocks, width, DN_SPLIT) * mask[:, None, split]
            result = jnp.dot(
                mine[...], weight.reshape(hid, DN_SPLIT), preferred_element_type=F32
            )
            lanes = pl.ds(pl.multiple_of((tile % per) * DN_TILE + start, DN_SPLIT), DN_SPLIT)
            out_ref[tile // per, :, lanes] = result.astype(out_ref.dtype)

    def held_body(nth, carry):
        put(nth, held.at[nth])
        return carry

    def step_body(with_held, nth, carry):
        slot = lax.rem(nth, n_slots)
        if with_held:
            put(nth, held.at[nth])
        copy_of(nth, slot).wait()
        put(n_held + nth, buf.at[slot])

        @pl.when(nth + n_slots < streamed)
        def _():
            copy_of(nth + n_slots, slot).start()

        return carry

    both = min(n_held, streamed)
    if both < n_held:
        lax.fori_loop(both, n_held, held_body, 0)
    if both:
        lax.fori_loop(0, both, functools.partial(step_body, True), 0)
    if both < streamed:
        lax.fori_loop(both, streamed, functools.partial(step_body, False), 0)
    if last:
        passed = pass_ref.shape[0]
        pass_ref[...] = out_ref[pl.ds(0, passed)].astype(BF)
        out_ref[passed] += x_ref[:, pl.ds(0, cols)].astype(F32)


def down(part, me, take, inner, x_own, masks, held, w_down):
    hid, depth = w_down.shape[1:]
    rows = x_own.shape[0]
    cols = depth // 8
    pieces = len(DN_PARTS[part])
    n_held = held[0].shape[0] if held else 0
    out = [jax.ShapeDtypeStruct((pieces, rows, cols), F32 if part else BF)]
    if part == 0:
        out.append(jax.ShapeDtypeStruct((rows, hid), BF))
    if part == len(DN_PARTS) - 1:
        out.append(jax.ShapeDtypeStruct((pieces // 2, rows, cols), BF))
    return pl.pallas_call(
        functools.partial(down_kernel, part, n_held),
        in_specs=[SM, SM, VM, VM, VM] + [VM] * len(held) + [HB],
        out_specs=(VM,) * len(out),
        out_shape=tuple(out),
        scratch_shapes=[
            pltpu.VMEM((DN_SLOTS, hid, DN_TILE), BF),
            pltpu.SemaphoreType.DMA((DN_SLOTS,)),
        ],
        compiler_params=pltpu.CompilerParams(vmem_limit_bytes=9 * MIB),
        cost_estimate=pl.CostEstimate(
            flops=2 * rows * pieces * cols * hid,
            bytes_accessed=2 * (pieces * cols - n_held * DN_TILE) * hid,
            transcendentals=0,
        ),
        name="down",
    )(me, take, inner, x_own, masks, *held, w_down)


def partner(block, distance):
    devices = range(lax.axis_size("tp"))
    return lax.ppermute(block, "tp", [(i, i ^ distance) for i in devices])


def onward(block, distance):
    tp_count = lax.axis_size("tp")
    sections = lax.axis_size("section")
    route = [
        (s * tp_count + t, (s + 1) % sections * tp_count + (t ^ distance))
        for s in range(sections)
        for t in range(tp_count)
    ]
    return lax.ppermute(block, ("section", "tp"), route)


def beside_exchanged(blocks):
    chips = blocks.shape[0] // 2
    return jnp.concatenate([blocks[:chips], partner(blocks[chips:], 1)], axis=2)


def along_exchanged(both):
    far_first = [partner(both[k], 2 * k) for k in range(both.shape[0] - 1, 0, -1)]
    return [both[0]] + far_first[::-1]


def sorted_arrivals(got):
    got = jnp.stack(got)
    share = got.shape[2] // 2
    return jnp.concatenate([got[:, :, :share], got[:, :, share:]])


def line_of_eight(
    tokens,
    norm_gain,
    gate_weight,
    up_weight,
    gate_mask,
    up_mask,
    down_weight,
    down_mask,
    slot_order,
):
    sections = lax.axis_size("section")
    tp_count = lax.axis_size("tp")
    section_pos = lax.axis_index("section")
    tp_pos = lax.axis_index("tp")
    rows, cols = tokens.shape
    my_blocks = slot_order[0]
    per_device = my_blocks.shape[0]
    chips = tp_count // 2
    me = tp_pos.astype(jnp.int32).reshape(1)

    gate_weight, up_weight, down_weight = (
        pltpu.with_memory_space_constraint(w, pltpu.HBM)
        for w in (gate_weight, up_weight, down_weight)
    )
    numbers = jnp.pad(my_blocks, (0, 128 - per_device)).astype(BF)
    own = jnp.concatenate([tokens, jnp.broadcast_to(numbers[None], (rows, 128))], axis=1)
    send = jnp.zeros((per_device,), jnp.int32)
    gu_masks, dn_masks, norm_gain = spread_masks(
        gate_mask[0].T,
        up_mask[0].T,
        down_mask[0],
        norm_gain,
        gate_weight.shape[2],
        down_weight.shape[2],
    )
    gu_held = [[]] * len(GU_HELD)
    saved = jnp.zeros(tokens.shape, BF)
    for round_pos in range(sections):
        straight = [partner(own, 2 * k) for k in range(chips - 1, 0, -1)]
        beside = partner(own, 1)
        arrivals = gate_up(
            0, me, send, norm_gain, gu_masks, [own[None], beside[None]], [], gu_held[0],
            gate_weight, up_weight,
        )
        if round_pos:
            straight[0], arrivals = lax.optimization_barrier((straight[0], arrivals))
            arrivals = gate_up(
                1, me, send, norm_gain, gu_masks, [straight[0][None]], arrivals, gu_held[1],
                gate_weight, up_weight,
            )
        straight, arrivals = lax.optimization_barrier((straight, arrivals))
        near = jnp.stack(straight)
        far = partner(near, 1)
        part = 2 if round_pos else GU_FIRST_ROUND
        arrivals = gate_up(
            part, me, send, norm_gain, gu_masks,
            [x[None] for x in straight[-len(GU_PARTS[part]) :]], arrivals,
            gu_held[part], gate_weight, up_weight,
        )
        far, arrivals = lax.optimization_barrier((far, arrivals))
        if round_pos == 0:
            send, take = slots(
                me, [own[None], near, beside[None], far], ((0,), (3, 2, 1), (4,), (7, 6, 5)),
                cols, per_device,
            )
        blocks = gate_up(
            3, me, send, norm_gain, gu_masks, [far], arrivals, gu_held[3],
            gate_weight, up_weight,
        )
        both, turn = lax.optimization_barrier((beside_exchanged(blocks), me))
        dn_held = hold(DN_PARTS, DN_HELD, turn, (down_weight,))
        got, dn_held = lax.optimization_barrier((along_exchanged(both), dn_held))
        dn_held = [[tiles] for tiles in dn_held]
        arrived = sorted_arrivals(got)
        passed, mine = down(0, me, take, arrived, own, dn_masks, dn_held[0], down_weight)
        got = partner(passed, 1).astype(F32)
        (kept,) = down(1, me, take, mine, own, dn_masks, dn_held[1], down_weight)
        outward, mine = lax.optimization_barrier(((kept + got).astype(BF), mine))
        nearer = partner(outward, 2)
        kept, passed = down(2, me, take, mine, own, dn_masks, dn_held[2], down_weight)
        nearer, kept, passed = lax.optimization_barrier((nearer, kept, passed))
        sums = kept[2:] + partner(passed, 1).astype(F32) + nearer.astype(F32)
        sums = sums.astype(BF)
        sums, turn = lax.optimization_barrier((sums, me))
        parts = GU_BROUGHT if round_pos else GU_BROUGHT + GU_STAYING
        halves = [onward(sums[0], 0), onward(sums[1], 4)]
        if round_pos + 1 < sections:
            tiles = hold(
                tuple(GU_PARTS[part] for part in parts),
                tuple(GU_HELD[part] for part in parts),
                turn,
                (gate_weight, up_weight),
            )
            halves, tiles = lax.optimization_barrier((halves, tiles))
            for part, held in zip(parts, tiles):
                gu_held[part] = [held]
        own = (halves[0].astype(F32) + halves[1].astype(F32)).astype(BF)
        saved = jnp.where(section_pos == (round_pos + 1) % sections, own, saved)
    return saved[None]


def solution(mesh):
    tp_count = mesh.shape["tp"]
    line_body = line_of_eight if tp_count == 8 else ring_body
    return jax.shard_map(
        line_body,
        mesh=mesh,
        in_specs=(
            P(None, "tp"),
            P("section", None),
            P("section", None, "tp"),
            P("section", None, "tp"),
            P("section", None, "tp"),
            P("section", None, "tp"),
            P("section", "tp", None),
            P("section", "tp", None),
            P("section", "tp"),
        ),
        out_specs=P("section", None, "tp"),
        check_vma=False,
    )
```

```python
import functools

import jax
import jax.numpy as jnp
from jax import lax
from jax.experimental import pallas as pl
from jax.experimental.pallas import tpu as pltpu
from jax.sharding import PartitionSpec as P


def passed_along(block, axis, distance):
    devices = range(lax.axis_size(axis))
    route = [((i - distance) % len(devices), i) for i in devices]
    return lax.ppermute(block, axis, route)


def expand_mask(mask, width):
    return jnp.repeat(jnp.repeat(mask, width, axis=0), width, axis=1)


def masked(weight, mask, width):
    return weight * expand_mask(mask, width).astype(jnp.bfloat16)


def ring_body(
    tokens,
    norm_gain,
    gate_weight,
    up_weight,
    gate_mask,
    up_mask,
    down_weight,
    down_mask,
    slot_order,
):
    sections = lax.axis_size("section")
    tp_count = lax.axis_size("tp")
    section_pos = lax.axis_index("section")
    tp_pos = lax.axis_index("tp")
    width = gate_weight.shape[1] // gate_mask.shape[1]
    w_gate = masked(gate_weight[0], gate_mask[0], width)
    w_up = masked(up_weight[0], up_mask[0], width)
    w_down = masked(down_weight[0], down_mask[0], width)
    gain = norm_gain[0]
    my_blocks = slot_order[0]
    per_device = my_blocks.shape[0]
    row_count, own_cols = tokens.shape
    window = min(tp_count, per_device)
    capacity = per_device // window
    slot_ids = jnp.arange(capacity, dtype=jnp.int32)
    my_source = my_blocks // per_device
    my_offset = (my_source - tp_pos) % tp_count
    lanes = jnp.arange(per_device, dtype=jnp.int32)
    earlier = (my_source[None, :] == my_source[:, None]) & (lanes[None, :] < lanes[:, None])
    my_rank = jnp.sum(earlier.astype(jnp.int32), axis=1)
    send_lists = []
    for offset in range(window):
        if offset == 0:
            table_row = my_blocks
        else:
            table_row = passed_along(my_blocks, "tp", offset)
        row_source = table_row // per_device
        row_block = table_row % per_device
        from_me = (row_source == tp_pos).astype(jnp.int32)
        order_rank = jnp.cumsum(from_me) - 1
        picks = (from_me[None, :] == 1) & (order_rank[None, :] == slot_ids[:, None])
        send_lists.append(jnp.sum(jnp.where(picks, row_block[None, :], 0), axis=1))
    x_full = lax.all_gather(tokens, "tp", axis=1, tiled=True)
    saved = jnp.zeros((row_count, own_cols), jnp.bfloat16)
    for round_pos in range(sections):
        x_own = lax.dynamic_slice_in_dim(x_full, tp_pos * own_cols, own_cols, 1)
        widened = x_full.astype(jnp.float32)
        scale = lax.rsqrt(jnp.mean(widened * widened, axis=-1, keepdims=True) + 1e-05)
        normed = (widened * scale * gain).astype(jnp.bfloat16)
        gate = jnp.dot(normed, w_gate, preferred_element_type=jnp.float32)
        upper = jnp.dot(normed, w_up, preferred_element_type=jnp.float32)
        hidden = (jax.nn.silu(gate) * upper).astype(jnp.bfloat16)
        flat = (
            hidden.reshape(row_count, per_device, width)
            .transpose(1, 0, 2)
            .reshape(per_device, row_count * width)
        )
        arrivals = []
        for gather_offset in range(window):
            outgoing = flat[send_lists[gather_offset]]
            if gather_offset == 0:
                arrivals.append(outgoing)
            else:
                arrivals.append(passed_along(outgoing, "tp", tp_count - gather_offset))
        stacked = jnp.stack(arrivals)
        chosen = stacked[my_offset, my_rank]
        mine = (
            chosen.reshape(per_device, row_count, width)
            .transpose(1, 0, 2)
            .reshape(row_count, per_device * width)
        )
        partial_sum = jnp.dot(mine, w_down, preferred_element_type=jnp.float32)
        summed = lax.psum_scatter(partial_sum, "tp", scatter_dimension=1, tiled=True)
        y_own = (x_own.astype(jnp.float32) + summed).astype(jnp.bfloat16)
        got_own = passed_along(y_own, "section", 1)
        if round_pos + 1 < sections:
            x_full = lax.all_gather(got_own, "tp", axis=1, tiled=True)
        saved = jnp.where(section_pos == (round_pos + 1) % sections, got_own, saved)
    return saved[None]


BF = jnp.bfloat16
F32 = jnp.float32
VM = pl.BlockSpec(memory_space=pltpu.VMEM)
SM = pl.BlockSpec(memory_space=pltpu.SMEM)
HB = pl.BlockSpec(memory_space=pltpu.HBM)
MIB = 2**20


def place(load_pair, first, second):
    lanes = lax.broadcasted_iota(jnp.int32, (1, 128), 1)
    left = pltpu.roll(load_pair(first // 2), 64 * (first % 2), 1)
    right = pltpu.roll(load_pair(second // 2), 64 * (1 - second % 2), 1)
    return jnp.where(lanes < 64, left, right).astype(BF)


GU_TILE, DN_TILE = 512, 512
GU_SLOTS, DN_SLOTS = 3, 3
GU_SPLIT, DN_SPLIT = 512, 256
GU_PARTS = ((0, 4), (3,), (2, 1), (7, 6, 5), (3, 2, 1))
GU_HELD = (2, 1, 2, 3, 0)
DN_PARTS = ((5, 7), (1, 3), (4, 6, 0, 2))
DN_HELD = (4, 4, 0)
GU_LAST, GU_FIRST_ROUND = 3, 4
GU_BROUGHT, GU_STAYING = (0, 1, 2), (3,)


def chosen(options, nth):
    value = options[0]
    for i, option in enumerate(options[1:]):
        value = jnp.where(nth == i + 1, option, value)
    return value


def place_of(me, piece):
    return me ^ (piece // 4 + 2 * (piece % 4))


def gate_up_row(me, pieces, cols, tile):
    per = cols // GU_TILE
    row = place_of(me, chosen(pieces, tile // per)) * cols + (tile % per) * GU_TILE
    return pl.multiple_of(row, GU_TILE)


def down_col(me, pieces, cols, tile):
    per = cols // DN_TILE
    col = place_of(me, chosen(pieces, tile // per)) * cols + (tile % per) * DN_TILE
    return pl.multiple_of(col, DN_TILE)


def spread_of(start, blocks, columns, width):
    return (
        lax.broadcasted_iota(jnp.int32, (blocks, columns), 0)
        == (start + lax.broadcasted_iota(jnp.int32, (blocks, columns), 1)) // width
    ).astype(BF)


def masks_kernel(gm, um, dm, gain, gu_masks, dn_masks, gain_ref, gm_ref, um_ref, dm_ref, sem):
    pairs = ((gm, gm_ref), (um, um_ref), (dm, dm_ref), (gain, gain_ref))
    copies = [pltpu.make_async_copy(src, dst, sem.at[n]) for n, (src, dst) in enumerate(pairs)]
    for copy in copies:
        copy.start()
    hid = gu_masks.shape[2]
    blocks = gm_ref.shape[0]
    spread = spread_of(0, blocks, hid, hid // blocks)
    for copy in copies:
        copy.wait()
    for j, mask in enumerate((gm_ref, um_ref)):
        gu_masks[j] = lax.dot_general(
            mask[...].astype(F32).astype(BF),
            spread,
            (((0,), (0,)), ((), ())),
            preferred_element_type=F32,
        )
    per = hid // DN_TILE
    for start in range(0, dm_ref.shape[1], blocks):
        mask = dm_ref[:, start : start + blocks].astype(F32).astype(BF)
        wide = jnp.dot(mask, spread, preferred_element_type=F32)
        for i in range(per):
            dn_masks[start // blocks * per + i] = wide[:, i * DN_TILE : (i + 1) * DN_TILE]


def spread_masks(gate_mask, up_mask, down_mask, gain, hid, depth):
    operands = [
        pltpu.with_memory_space_constraint(x, pltpu.HBM)
        for x in (gate_mask, up_mask, down_mask, gain)
    ]
    return pl.pallas_call(
        masks_kernel,
        in_specs=[HB] * 4,
        out_specs=(VM, VM, VM),
        out_shape=(
            jax.ShapeDtypeStruct((2, gate_mask.shape[1], hid), F32),
            jax.ShapeDtypeStruct((depth // DN_TILE, down_mask.shape[0], DN_TILE), F32),
            jax.ShapeDtypeStruct(gain.shape, F32),
        ),
        scratch_shapes=[pltpu.VMEM(x.shape, jnp.int32) for x in operands[:3]]
        + [pltpu.SemaphoreType.DMA((4,))],
        compiler_params=pltpu.CompilerParams(vmem_limit_bytes=4 * MIB),
        name="spread_masks",
    )(*operands)


def owner_and_place(block, per_device):
    if per_device & (per_device - 1):
        return lax.div(block, per_device), lax.rem(block, per_device)
    return block >> (per_device.bit_length() - 1), block & (per_device - 1)


def slots_kernel(cols, per_device, order, me_ref, *refs):
    x_refs, refs = refs[: len(order)], refs[len(order) :]
    send_ref, take_ref, table, orders, sem, found, count = refs
    me = me_ref[0]
    for x_ref, places in zip(x_refs, order):
        for i, piece in enumerate(places):
            row = x_ref[i, pl.ds(0, 16), pl.ds(cols, 128)].astype(F32)[0:1]
            table[pl.ds(piece, 1), :] = row.astype(jnp.int32)
    copy = pltpu.make_async_copy(table, orders, sem)
    copy.start()
    copy.wait()
    pieces = orders.shape[0]
    capacity = per_device // pieces

    def send_body(slot, ranks):
        after = []
        for piece, rank in enumerate(ranks):
            block = orders[piece, slot]
            owner, at = owner_and_place(block, per_device)
            found[piece * (capacity + 1) + rank] = at
            after.append(rank + (owner == me).astype(jnp.int32))
        return tuple(after)

    lax.fori_loop(0, per_device, send_body, (jnp.int32(0),) * pieces, unroll=2)
    for piece in range(pieces):
        count[piece] = 0
        for rank in range(capacity):
            send_ref[piece * capacity + rank] = found[piece * (capacity + 1) + rank]

    def take_body(slot, carry):
        apart = owner_and_place(orders[0, slot], per_device)[0] ^ me
        piece = (apart & 1) * (pieces // 2) + (apart >> 1)
        rank = count[piece]
        take_ref[slot] = piece * capacity + rank
        count[piece] = rank + 1
        return carry

    lax.fori_loop(0, per_device, take_body, 0)


def slots(me, xs, order, cols, per_device):
    pieces = sum(len(places) for places in order)
    table = jax.ShapeDtypeStruct((per_device,), jnp.int32)
    return pl.pallas_call(
        functools.partial(slots_kernel, cols, per_device, order),
        in_specs=[SM] + [VM] * len(xs),
        out_specs=(SM, SM),
        out_shape=(table, table),
        scratch_shapes=[
            pltpu.VMEM((pieces, 128), jnp.int32),
            pltpu.SMEM((pieces, 128), jnp.int32),
            pltpu.SemaphoreType.DMA,
            pltpu.SMEM((per_device + pieces,), jnp.int32),
            pltpu.SMEM((pieces,), jnp.int32),
        ],
        compiler_params=pltpu.CompilerParams(vmem_limit_bytes=MIB),
        name="slots",
    )(me, *xs)


def hold_kernel(parts, me_ref, *refs):
    me = me_ref[0]
    sem = refs[-1]
    weights, held_refs = refs[: -1 - len(parts)], refs[-1 - len(parts) : -1]
    pairs = []
    for pieces, ref in zip(parts, held_refs):
        for tile in range(ref.shape[0]):
            if len(weights) == 2:
                row = gate_up_row(me, pieces, weights[0].shape[1] // 8, tile)
                for j, w in enumerate(weights):
                    pairs.append((w.at[0, pl.ds(row, GU_TILE)], ref.at[tile, j]))
            else:
                col = down_col(me, pieces, weights[0].shape[2] // 8, tile)
                pairs.append((weights[0].at[0, :, pl.ds(col, DN_TILE)], ref.at[tile]))
    copies = [pltpu.make_async_copy(src, dst, sem.at[n]) for n, (src, dst) in enumerate(pairs)]
    for copy in copies:
        copy.start()
    for copy in copies:
        copy.wait()


def hold(parts, counts, me, weights):
    if len(weights) == 2:
        shapes = [(n, 2, GU_TILE, weights[0].shape[2]) for n in counts]
    else:
        shapes = [(n, weights[0].shape[1], DN_TILE) for n in counts]
    shapes = [jax.ShapeDtypeStruct(shape, BF) for shape in shapes]
    return pl.pallas_call(
        functools.partial(hold_kernel, parts),
        in_specs=[SM] + [HB] * len(weights),
        out_specs=(VM,) * len(shapes),
        out_shape=tuple(shapes),
        scratch_shapes=[pltpu.SemaphoreType.DMA((len(weights) * sum(counts),))],
        compiler_params=pltpu.CompilerParams(vmem_limit_bytes=2 * MIB),
        cost_estimate=pl.CostEstimate(
            flops=0, bytes_accessed=sum(2 * x.size for x in shapes), transcendentals=0
        ),
        name="hold",
    )(me, *weights)


def held_parts(parts, me, w_gate, w_up):
    return hold(
        tuple(GU_PARTS[part] for part in parts),
        tuple(GU_HELD[part] for part in parts),
        me,
        (w_gate, w_up),
    )


def gate_up_kernel(part, n_x, n_before, n_held, me_ref, send_ref, gain_ref, masks, *refs):
    pieces = GU_PARTS[part]
    last = part == GU_LAST
    x_refs, refs = refs[:n_x], refs[n_x:]
    before, refs = refs[: 2 * n_before], refs[2 * n_before :]
    if n_held:
        held, refs = refs[0], refs[1:]
    wg, wu = refs[:2]
    if last:
        out_ref, buf, sem, scaled, acc = refs[2:]
    else:
        acc, sq_ref, buf, sem, scaled = refs[2:]
    rows, cols = scaled.shape[1:]
    depth, hid = wg.shape[1:]
    width = depth // masks.shape[1]
    per = cols // GU_TILE
    kept = GU_TILE // width
    streamed = len(pieces) * per - n_held
    me = me_ref[0]

    def copies(nth, slot):
        row = gate_up_row(me, pieces, cols, n_held + nth)
        return [
            pltpu.make_async_copy(
                w.at[0, pl.ds(row, GU_TILE)], buf.at[slot, j], sem.at[slot, j]
            )
            for j, w in enumerate((wg, wu))
        ]

    slots = min(GU_SLOTS, streamed)
    for nth in range(slots):
        for copy in copies(nth, nth):
            copy.start()
    squares = jnp.zeros((rows, 128), F32)
    at = 0
    for x_ref in x_refs:
        for i in range(x_ref.shape[0]):
            start = pl.multiple_of(place_of(me, pieces[at]) * cols, cols)
            wide = x_ref[i, :, pl.ds(0, cols)].astype(F32)
            for lane in range(0, cols, 128):
                squares = squares + wide[:, lane : lane + 128] * wide[:, lane : lane + 128]
            scaled[at] = (wide * gain_ref[:, pl.ds(start, cols)]).astype(BF)
            at += 1
    if n_before:
        for j in range(2):
            total = before[0][j]
            for i in range(1, n_before):
                total = total + before[2 * i][j]
            acc[j] = total
        for i in range(n_before):
            squares = squares + before[2 * i + 1][...]
    else:
        acc[...] = jnp.zeros_like(acc)

    def add_product(tile, j, weight_ref):
        lanes = pl.ds(pl.multiple_of((tile % per) * GU_TILE, GU_TILE), GU_TILE)
        x_part = scaled[tile // per, :, lanes]
        row = gate_up_row(me, pieces, cols, tile)
        mask = masks[j, pl.ds(pl.multiple_of(row // width, kept), kept), :].astype(BF)
        for start in range(0, hid, GU_SPLIT):
            split = slice(start, start + GU_SPLIT)
            weight = weight_ref[:, split].reshape(kept, width, GU_SPLIT) * mask[:, None, split]
            acc[j, :, split] += jnp.dot(
                x_part, weight.reshape(GU_TILE, GU_SPLIT), preferred_element_type=F32
            )

    def step_body(with_held, nth, carry):
        slot = lax.rem(nth, slots)
        for j, copy in enumerate(copies(nth, slot)):
            if with_held:
                add_product(nth, j, held.at[nth, j])
            copy.wait()
            add_product(n_held + nth, j, buf.at[slot, j])

        @pl.when(nth + slots < streamed)
        def _():
            for copy in copies(nth + slots, slot):
                copy.start()

        return carry

    def held_body(nth, carry):
        for j in range(2):
            add_product(nth, j, held.at[nth, j])
        return carry

    both = min(n_held, streamed)
    if both < n_held:
        lax.fori_loop(both, n_held, held_body, 0)
    if both:
        lax.fori_loop(0, both, functools.partial(step_body, True), 0)
    if both < streamed:
        lax.fori_loop(both, streamed, functools.partial(step_body, False), 0)
    if not last:
        sq_ref[...] = squares
        return
    scale = lax.rsqrt(jnp.sum(squares, axis=1, keepdims=True) / depth + 1e-05)
    gate = acc[0] * scale
    hidden = (gate / (1.0 + jnp.exp(-gate)) * (acc[1] * scale)).astype(BF)
    acc[0] = hidden.astype(F32)

    def load_pair(pair):
        return acc[0, :, pl.ds(pl.multiple_of(pair * 128, 128), 128)]

    each = out_ref.shape[2] // 128
    for piece in range(out_ref.shape[0]):
        for pair in range(each):
            at = piece * 2 * each + 2 * pair
            out_ref[piece, :, pl.ds(pair * 128, 128)] = place(
                load_pair, send_ref[at], send_ref[at + 1]
            )


def gate_up(part, me, send, gain, masks, xs, before, held, w_gate, w_up):
    rows = xs[0].shape[1]
    depth, hid = w_gate.shape[1:]
    cols = depth // 8
    pieces = len(GU_PARTS[part])
    last = part == GU_LAST
    acc = (2, rows, hid)
    scratch = [
        pltpu.VMEM((GU_SLOTS, 2, GU_TILE, hid), BF),
        pltpu.SemaphoreType.DMA((GU_SLOTS, 2)),
        pltpu.VMEM((pieces, rows, cols), BF),
    ]
    if last:
        out_specs, out_shape = VM, jax.ShapeDtypeStruct((8, rows, hid // 8), BF)
        scratch.append(pltpu.VMEM(acc, F32))
    else:
        out_specs = (VM, VM)
        out_shape = (jax.ShapeDtypeStruct(acc, F32), jax.ShapeDtypeStruct((rows, 128), F32))
    operands = list(xs) + list(before) + list(held)
    n_held = held[0].shape[0] if held else 0
    return pl.pallas_call(
        functools.partial(gate_up_kernel, part, len(xs), len(before) // 2, n_held),
        in_specs=[SM, SM, VM, VM] + [VM] * len(operands) + [HB, HB],
        out_specs=out_specs,
        out_shape=out_shape,
        scratch_shapes=scratch,
        compiler_params=pltpu.CompilerParams(vmem_limit_bytes=15 * MIB),
        cost_estimate=pl.CostEstimate(
            flops=4 * rows * pieces * cols * hid,
            bytes_accessed=4 * (pieces * cols - n_held * GU_TILE) * hid,
            transcendentals=0,
        ),
        name="gate_up",
    )(me, send, gain, masks, *operands, w_gate, w_up)


def down_kernel(part, n_held, me_ref, take_ref, inner_ref, x_ref, masks, *refs):
    pieces = DN_PARTS[part]
    if n_held:
        held, refs = refs[0], refs[1:]
    wd, refs = refs[0], refs[1:]
    first, last = part == 0, part == len(DN_PARTS) - 1
    if first:
        out_ref, mine, buf, sem = refs
    elif last:
        out_ref, pass_ref, buf, sem = refs
    else:
        out_ref, buf, sem = refs
    if not first:
        mine = inner_ref
    hid, depth = wd.shape[1:]
    cols = depth // 8
    blocks = masks.shape[1]
    width = hid // blocks
    per = cols // DN_TILE
    streamed = len(pieces) * per - n_held
    n_slots = min(DN_SLOTS, streamed)
    me = me_ref[0]

    def copy_of(nth, slot):
        col = down_col(me, pieces, cols, n_held + nth)
        return pltpu.make_async_copy(wd.at[0, :, pl.ds(col, DN_TILE)], buf.at[slot], sem.at[slot])

    for nth in range(n_slots):
        copy_of(nth, nth).start()
    if first:
        each = inner_ref.shape[2] // 128

        def load_pair(pair):
            lane = pl.multiple_of((pair % each) * 128, 128)
            return inner_ref[pair // each, :, pl.ds(lane, 128)].astype(F32)

        for pair in range(hid // 128):
            mine[:, pl.ds(pair * 128, 128)] = place(
                load_pair, take_ref[2 * pair], take_ref[2 * pair + 1]
            )

    def put(tile, weight_ref):
        mask = masks[down_col(me, pieces, cols, tile) // DN_TILE].astype(BF)
        for start in range(0, DN_TILE, DN_SPLIT):
            split = slice(start, start + DN_SPLIT)
            weight = weight_ref[:, split].reshape(blocks, width, DN_SPLIT) * mask[:, None, split]
            result = jnp.dot(
                mine[...], weight.reshape(hid, DN_SPLIT), preferred_element_type=F32
            )
            lanes = pl.ds(pl.multiple_of((tile % per) * DN_TILE + start, DN_SPLIT), DN_SPLIT)
            out_ref[tile // per, :, lanes] = result.astype(out_ref.dtype)

    def held_body(nth, carry):
        put(nth, held.at[nth])
        return carry

    def step_body(with_held, nth, carry):
        slot = lax.rem(nth, n_slots)
        if with_held:
            put(nth, held.at[nth])
        copy_of(nth, slot).wait()
        put(n_held + nth, buf.at[slot])

        @pl.when(nth + n_slots < streamed)
        def _():
            copy_of(nth + n_slots, slot).start()

        return carry

    both = min(n_held, streamed)
    if both < n_held:
        lax.fori_loop(both, n_held, held_body, 0)
    if both:
        lax.fori_loop(0, both, functools.partial(step_body, True), 0)
    if both < streamed:
        lax.fori_loop(both, streamed, functools.partial(step_body, False), 0)
    if last:
        passed = pass_ref.shape[0]
        pass_ref[...] = out_ref[pl.ds(0, passed)].astype(BF)
        out_ref[passed] += x_ref[:, pl.ds(0, cols)].astype(F32)


def down(part, me, take, inner, x_own, masks, held, w_down):
    hid, depth = w_down.shape[1:]
    rows = x_own.shape[0]
    cols = depth // 8
    pieces = len(DN_PARTS[part])
    n_held = held[0].shape[0] if held else 0
    out = [jax.ShapeDtypeStruct((pieces, rows, cols), F32 if part else BF)]
    if part == 0:
        out.append(jax.ShapeDtypeStruct((rows, hid), BF))
    if part == len(DN_PARTS) - 1:
        out.append(jax.ShapeDtypeStruct((pieces // 2, rows, cols), BF))
    return pl.pallas_call(
        functools.partial(down_kernel, part, n_held),
        in_specs=[SM, SM, VM, VM, VM] + [VM] * len(held) + [HB],
        out_specs=(VM,) * len(out),
        out_shape=tuple(out),
        scratch_shapes=[
            pltpu.VMEM((DN_SLOTS, hid, DN_TILE), BF),
            pltpu.SemaphoreType.DMA((DN_SLOTS,)),
        ],
        compiler_params=pltpu.CompilerParams(vmem_limit_bytes=9 * MIB),
        cost_estimate=pl.CostEstimate(
            flops=2 * rows * pieces * cols * hid,
            bytes_accessed=2 * (pieces * cols - n_held * DN_TILE) * hid,
            transcendentals=0,
        ),
        name="down",
    )(me, take, inner, x_own, masks, *held, w_down)


def partner(block, distance):
    devices = range(lax.axis_size("tp"))
    return lax.ppermute(block, "tp", [(i, i ^ distance) for i in devices])


def onward(block, distance):
    tp_count = lax.axis_size("tp")
    sections = lax.axis_size("section")
    route = [
        (s * tp_count + t, (s + 1) % sections * tp_count + (t ^ distance))
        for s in range(sections)
        for t in range(tp_count)
    ]
    return lax.ppermute(block, ("section", "tp"), route)


def beside_exchanged(blocks):
    chips = blocks.shape[0] // 2
    return jnp.concatenate([blocks[:chips], partner(blocks[chips:], 1)], axis=2)


def along_exchanged(both):
    far_first = [partner(both[k], 2 * k) for k in range(both.shape[0] - 1, 0, -1)]
    return [both[0]] + far_first[::-1]


def sorted_arrivals(got):
    got = jnp.stack(got)
    share = got.shape[2] // 2
    return jnp.concatenate([got[:, :, :share], got[:, :, share:]])


def line_of_eight(
    tokens,
    norm_gain,
    gate_weight,
    up_weight,
    gate_mask,
    up_mask,
    down_weight,
    down_mask,
    slot_order,
):
    sections = lax.axis_size("section")
    tp_count = lax.axis_size("tp")
    section_pos = lax.axis_index("section")
    tp_pos = lax.axis_index("tp")
    rows, cols = tokens.shape
    my_blocks = slot_order[0]
    per_device = my_blocks.shape[0]
    chips = tp_count // 2
    me = tp_pos.astype(jnp.int32).reshape(1)

    gate_weight, up_weight, down_weight = (
        pltpu.with_memory_space_constraint(w, pltpu.HBM)
        for w in (gate_weight, up_weight, down_weight)
    )
    numbers = jnp.pad(my_blocks, (0, 128 - per_device)).astype(BF)
    own = jnp.concatenate([tokens, jnp.broadcast_to(numbers[None], (rows, 128))], axis=1)
    send = jnp.zeros((per_device,), jnp.int32)
    gu_masks, dn_masks, norm_gain = spread_masks(
        gate_mask[0].T,
        up_mask[0].T,
        down_mask[0],
        norm_gain,
        gate_weight.shape[2],
        down_weight.shape[2],
    )
    gu_held = [[]] * len(GU_HELD)
    saved = jnp.zeros(tokens.shape, BF)
    for round_pos in range(sections):
        straight = [partner(own, 2 * k) for k in range(chips - 1, 0, -1)]
        beside = partner(own, 1)
        arrivals = gate_up(
            0, me, send, norm_gain, gu_masks, [own[None], beside[None]], [], gu_held[0],
            gate_weight, up_weight,
        )
        if round_pos:
            straight[0], arrivals = lax.optimization_barrier((straight[0], arrivals))
            arrivals = gate_up(
                1, me, send, norm_gain, gu_masks, [straight[0][None]], arrivals, gu_held[1],
                gate_weight, up_weight,
            )
        straight, arrivals = lax.optimization_barrier((straight, arrivals))
        near = jnp.stack(straight)
        far = partner(near, 1)
        part = 2 if round_pos else GU_FIRST_ROUND
        arrivals = gate_up(
            part, me, send, norm_gain, gu_masks,
            [x[None] for x in straight[-len(GU_PARTS[part]) :]], arrivals,
            gu_held[part], gate_weight, up_weight,
        )
        far, arrivals = lax.optimization_barrier((far, arrivals))
        if round_pos == 0:
            send, take = slots(
                me, [own[None], near, beside[None], far], ((0,), (3, 2, 1), (4,), (7, 6, 5)),
                cols, per_device,
            )
        blocks = gate_up(
            3, me, send, norm_gain, gu_masks, [far], arrivals, gu_held[3],
            gate_weight, up_weight,
        )
        both, turn = lax.optimization_barrier((beside_exchanged(blocks), me))
        parts = [part for part, count in enumerate(DN_HELD) if count]
        tiles = hold(
            tuple(DN_PARTS[part] for part in parts),
            tuple(DN_HELD[part] for part in parts),
            turn,
            (down_weight,),
        )
        got, tiles = lax.optimization_barrier((along_exchanged(both), tiles))
        dn_held = [[]] * len(DN_HELD)
        for part, held in zip(parts, tiles):
            dn_held[part] = [held]
        arrived = sorted_arrivals(got)
        passed, mine = down(0, me, take, arrived, own, dn_masks, dn_held[0], down_weight)
        got = partner(passed, 1).astype(F32)
        (kept,) = down(1, me, take, mine, own, dn_masks, dn_held[1], down_weight)
        outward, mine = lax.optimization_barrier(((kept + got).astype(BF), mine))
        nearer = partner(outward, 2)
        kept, passed = down(2, me, take, mine, own, dn_masks, dn_held[2], down_weight)
        nearer, kept, passed = lax.optimization_barrier((nearer, kept, passed))
        sums = kept[2:] + partner(passed, 1).astype(F32) + nearer.astype(F32)
        sums = sums.astype(BF)
        sums, turn = lax.optimization_barrier((sums, me))
        parts = GU_BROUGHT if round_pos else GU_BROUGHT + GU_STAYING
        far_half = onward(sums[1], 4)
        halves = [far_half, onward(sums[0], 0)]
        if round_pos + 1 < sections:
            tiles = held_parts(parts, turn, gate_weight, up_weight)
            halves, tiles = lax.optimization_barrier((halves, tiles))
            for part, held in zip(parts, tiles):
                gu_held[part] = [held]
        own = (halves[0].astype(F32) + halves[1].astype(F32)).astype(BF)
        saved = jnp.where(section_pos == (round_pos + 1) % sections, own, saved)
    return saved[None]


def solution(mesh):
    tp_count = mesh.shape["tp"]
    line_body = line_of_eight if tp_count == 8 else ring_body
    return jax.shard_map(
        line_body,
        mesh=mesh,
        in_specs=(
            P(None, "tp"),
            P("section", None),
            P("section", None, "tp"),
            P("section", None, "tp"),
            P("section", None, "tp"),
            P("section", None, "tp"),
            P("section", "tp", None),
            P("section", "tp", None),
            P("section", "tp"),
        ),
        out_specs=P("section", None, "tp"),
        check_vma=False,
    )
```

```python
import functools

import jax
import jax.numpy as jnp
from jax import lax
from jax.experimental import pallas as pl
from jax.experimental.pallas import tpu as pltpu
from jax.sharding import PartitionSpec as P


def passed_along(block, axis, distance):
    devices = range(lax.axis_size(axis))
    route = [((i - distance) % len(devices), i) for i in devices]
    return lax.ppermute(block, axis, route)


def expand_mask(mask, width):
    return jnp.repeat(jnp.repeat(mask, width, axis=0), width, axis=1)


def masked(weight, mask, width):
    return weight * expand_mask(mask, width).astype(jnp.bfloat16)


def ring_body(
    tokens,
    norm_gain,
    gate_weight,
    up_weight,
    gate_mask,
    up_mask,
    down_weight,
    down_mask,
    slot_order,
):
    sections = lax.axis_size("section")
    tp_count = lax.axis_size("tp")
    section_pos = lax.axis_index("section")
    tp_pos = lax.axis_index("tp")
    width = gate_weight.shape[1] // gate_mask.shape[1]
    w_gate = masked(gate_weight[0], gate_mask[0], width)
    w_up = masked(up_weight[0], up_mask[0], width)
    w_down = masked(down_weight[0], down_mask[0], width)
    gain = norm_gain[0]
    my_blocks = slot_order[0]
    per_device = my_blocks.shape[0]
    row_count, own_cols = tokens.shape
    window = min(tp_count, per_device)
    capacity = per_device // window
    slot_ids = jnp.arange(capacity, dtype=jnp.int32)
    my_source = my_blocks // per_device
    my_offset = (my_source - tp_pos) % tp_count
    lanes = jnp.arange(per_device, dtype=jnp.int32)
    earlier = (my_source[None, :] == my_source[:, None]) & (lanes[None, :] < lanes[:, None])
    my_rank = jnp.sum(earlier.astype(jnp.int32), axis=1)
    send_lists = []
    for offset in range(window):
        if offset == 0:
            table_row = my_blocks
        else:
            table_row = passed_along(my_blocks, "tp", offset)
        row_source = table_row // per_device
        row_block = table_row % per_device
        from_me = (row_source == tp_pos).astype(jnp.int32)
        order_rank = jnp.cumsum(from_me) - 1
        picks = (from_me[None, :] == 1) & (order_rank[None, :] == slot_ids[:, None])
        send_lists.append(jnp.sum(jnp.where(picks, row_block[None, :], 0), axis=1))
    x_full = lax.all_gather(tokens, "tp", axis=1, tiled=True)
    saved = jnp.zeros((row_count, own_cols), jnp.bfloat16)
    for round_pos in range(sections):
        x_own = lax.dynamic_slice_in_dim(x_full, tp_pos * own_cols, own_cols, 1)
        widened = x_full.astype(jnp.float32)
        scale = lax.rsqrt(jnp.mean(widened * widened, axis=-1, keepdims=True) + 1e-05)
        normed = (widened * scale * gain).astype(jnp.bfloat16)
        gate = jnp.dot(normed, w_gate, preferred_element_type=jnp.float32)
        upper = jnp.dot(normed, w_up, preferred_element_type=jnp.float32)
        hidden = (jax.nn.silu(gate) * upper).astype(jnp.bfloat16)
        flat = (
            hidden.reshape(row_count, per_device, width)
            .transpose(1, 0, 2)
            .reshape(per_device, row_count * width)
        )
        arrivals = []
        for gather_offset in range(window):
            outgoing = flat[send_lists[gather_offset]]
            if gather_offset == 0:
                arrivals.append(outgoing)
            else:
                arrivals.append(passed_along(outgoing, "tp", tp_count - gather_offset))
        stacked = jnp.stack(arrivals)
        chosen = stacked[my_offset, my_rank]
        mine = (
            chosen.reshape(per_device, row_count, width)
            .transpose(1, 0, 2)
            .reshape(row_count, per_device * width)
        )
        partial_sum = jnp.dot(mine, w_down, preferred_element_type=jnp.float32)
        summed = lax.psum_scatter(partial_sum, "tp", scatter_dimension=1, tiled=True)
        y_own = (x_own.astype(jnp.float32) + summed).astype(jnp.bfloat16)
        got_own = passed_along(y_own, "section", 1)
        if round_pos + 1 < sections:
            x_full = lax.all_gather(got_own, "tp", axis=1, tiled=True)
        saved = jnp.where(section_pos == (round_pos + 1) % sections, got_own, saved)
    return saved[None]


BF = jnp.bfloat16
F32 = jnp.float32
VM = pl.BlockSpec(memory_space=pltpu.VMEM)
SM = pl.BlockSpec(memory_space=pltpu.SMEM)
HB = pl.BlockSpec(memory_space=pltpu.HBM)
MIB = 2**20


def place(load_pair, first, second):
    lanes = lax.broadcasted_iota(jnp.int32, (1, 128), 1)
    left = pltpu.roll(load_pair(first // 2), 64 * (first % 2), 1)
    right = pltpu.roll(load_pair(second // 2), 64 * (1 - second % 2), 1)
    return jnp.where(lanes < 64, left, right).astype(BF)


GU_TILE, DN_TILE = 512, 512
GU_SLOTS, DN_SLOTS = 3, 3
GU_SPLIT, DN_SPLIT = 512, 256
GU_PARTS = ((0, 4), (3,), (2, 1), (7, 6, 5), (3, 2, 1))
GU_HELD = (0, 2, 2, 3, 0)
DN_PARTS = ((5, 7), (1, 3), (4, 6, 0, 2))
DN_HELD = (4, 4, 0)
GU_LAST, GU_FIRST_ROUND = 3, 4
GU_BROUGHT, GU_STAYING = (1, 2), (3,)


def chosen(options, nth):
    value = options[0]
    for i, option in enumerate(options[1:]):
        value = jnp.where(nth == i + 1, option, value)
    return value


def place_of(me, piece):
    return me ^ (piece // 4 + 2 * (piece % 4))


def gate_up_row(me, pieces, cols, tile):
    per = cols // GU_TILE
    row = place_of(me, chosen(pieces, tile // per)) * cols + (tile % per) * GU_TILE
    return pl.multiple_of(row, GU_TILE)


def down_col(me, pieces, cols, tile):
    per = cols // DN_TILE
    col = place_of(me, chosen(pieces, tile // per)) * cols + (tile % per) * DN_TILE
    return pl.multiple_of(col, DN_TILE)


def spread_of(start, blocks, columns, width):
    return (
        lax.broadcasted_iota(jnp.int32, (blocks, columns), 0)
        == (start + lax.broadcasted_iota(jnp.int32, (blocks, columns), 1)) // width
    ).astype(BF)


def masks_kernel(gm, um, dm, gain, gu_masks, dn_masks, gain_ref, gm_ref, um_ref, dm_ref, sem):
    pairs = ((gm, gm_ref), (um, um_ref), (dm, dm_ref), (gain, gain_ref))
    copies = [pltpu.make_async_copy(src, dst, sem.at[n]) for n, (src, dst) in enumerate(pairs)]
    for copy in copies:
        copy.start()
    hid = gu_masks.shape[2]
    blocks = gm_ref.shape[0]
    spread = spread_of(0, blocks, hid, hid // blocks)
    for copy in copies:
        copy.wait()
    for j, mask in enumerate((gm_ref, um_ref)):
        gu_masks[j] = lax.dot_general(
            mask[...].astype(F32).astype(BF),
            spread,
            (((0,), (0,)), ((), ())),
            preferred_element_type=F32,
        )
    per = hid // DN_TILE
    for start in range(0, dm_ref.shape[1], blocks):
        mask = dm_ref[:, start : start + blocks].astype(F32).astype(BF)
        wide = jnp.dot(mask, spread, preferred_element_type=F32)
        for i in range(per):
            dn_masks[start // blocks * per + i] = wide[:, i * DN_TILE : (i + 1) * DN_TILE]


def spread_masks(gate_mask, up_mask, down_mask, gain, hid, depth):
    operands = [
        pltpu.with_memory_space_constraint(x, pltpu.HBM)
        for x in (gate_mask, up_mask, down_mask, gain)
    ]
    return pl.pallas_call(
        masks_kernel,
        in_specs=[HB] * 4,
        out_specs=(VM, VM, VM),
        out_shape=(
            jax.ShapeDtypeStruct((2, gate_mask.shape[1], hid), F32),
            jax.ShapeDtypeStruct((depth // DN_TILE, down_mask.shape[0], DN_TILE), F32),
            jax.ShapeDtypeStruct(gain.shape, F32),
        ),
        scratch_shapes=[pltpu.VMEM(x.shape, jnp.int32) for x in operands[:3]]
        + [pltpu.SemaphoreType.DMA((4,))],
        compiler_params=pltpu.CompilerParams(vmem_limit_bytes=4 * MIB),
        name="spread_masks",
    )(*operands)


def owner_and_place(block, per_device):
    if per_device & (per_device - 1):
        return lax.div(block, per_device), lax.rem(block, per_device)
    return block >> (per_device.bit_length() - 1), block & (per_device - 1)


def slots_kernel(cols, per_device, order, me_ref, *refs):
    x_refs, refs = refs[: len(order)], refs[len(order) :]
    send_ref, take_ref, table, orders, sem, found, count = refs
    me = me_ref[0]
    for x_ref, places in zip(x_refs, order):
        for i, piece in enumerate(places):
            row = x_ref[i, pl.ds(0, 16), pl.ds(cols, 128)].astype(F32)[0:1]
            table[pl.ds(piece, 1), :] = row.astype(jnp.int32)
    copy = pltpu.make_async_copy(table, orders, sem)
    copy.start()
    copy.wait()
    pieces = orders.shape[0]
    capacity = per_device // pieces

    def send_body(slot, ranks):
        after = []
        for piece, rank in enumerate(ranks):
            block = orders[piece, slot]
            owner, at = owner_and_place(block, per_device)
            found[piece * (capacity + 1) + rank] = at
            after.append(rank + (owner == me).astype(jnp.int32))
        return tuple(after)

    lax.fori_loop(0, per_device, send_body, (jnp.int32(0),) * pieces, unroll=2)
    for piece in range(pieces):
        count[piece] = 0
        for rank in range(capacity):
            send_ref[piece * capacity + rank] = found[piece * (capacity + 1) + rank]

    def take_body(slot, carry):
        apart = owner_and_place(orders[0, slot], per_device)[0] ^ me
        piece = (apart & 1) * (pieces // 2) + (apart >> 1)
        rank = count[piece]
        take_ref[slot] = piece * capacity + rank
        count[piece] = rank + 1
        return carry

    lax.fori_loop(0, per_device, take_body, 0)


def slots(me, xs, order, cols, per_device):
    pieces = sum(len(places) for places in order)
    table = jax.ShapeDtypeStruct((per_device,), jnp.int32)
    return pl.pallas_call(
        functools.partial(slots_kernel, cols, per_device, order),
        in_specs=[SM] + [VM] * len(xs),
        out_specs=(SM, SM),
        out_shape=(table, table),
        scratch_shapes=[
            pltpu.VMEM((pieces, 128), jnp.int32),
            pltpu.SMEM((pieces, 128), jnp.int32),
            pltpu.SemaphoreType.DMA,
            pltpu.SMEM((per_device + pieces,), jnp.int32),
            pltpu.SMEM((pieces,), jnp.int32),
        ],
        compiler_params=pltpu.CompilerParams(vmem_limit_bytes=MIB),
        name="slots",
    )(me, *xs)


def hold_kernel(parts, me_ref, *refs):
    me = me_ref[0]
    sem = refs[-1]
    weights, held_refs = refs[: -1 - len(parts)], refs[-1 - len(parts) : -1]
    pairs = []
    for pieces, ref in zip(parts, held_refs):
        for tile in range(ref.shape[0]):
            if len(weights) == 2:
                row = gate_up_row(me, pieces, weights[0].shape[1] // 8, tile)
                for j, w in enumerate(weights):
                    pairs.append((w.at[0, pl.ds(row, GU_TILE)], ref.at[tile, j]))
            else:
                col = down_col(me, pieces, weights[0].shape[2] // 8, tile)
                pairs.append((weights[0].at[0, :, pl.ds(col, DN_TILE)], ref.at[tile]))
    copies = [pltpu.make_async_copy(src, dst, sem.at[n]) for n, (src, dst) in enumerate(pairs)]
    for copy in copies:
        copy.start()
    for copy in copies:
        copy.wait()


def hold(parts, counts, me, weights):
    if len(weights) == 2:
        shapes = [(n, 2, GU_TILE, weights[0].shape[2]) for n in counts]
    else:
        shapes = [(n, weights[0].shape[1], DN_TILE) for n in counts]
    shapes = [jax.ShapeDtypeStruct(shape, BF) for shape in shapes]
    return pl.pallas_call(
        functools.partial(hold_kernel, parts),
        in_specs=[SM] + [HB] * len(weights),
        out_specs=(VM,) * len(shapes),
        out_shape=tuple(shapes),
        scratch_shapes=[pltpu.SemaphoreType.DMA((len(weights) * sum(counts),))],
        compiler_params=pltpu.CompilerParams(vmem_limit_bytes=2 * MIB),
        cost_estimate=pl.CostEstimate(
            flops=0, bytes_accessed=sum(2 * x.size for x in shapes), transcendentals=0
        ),
        name="hold",
    )(me, *weights)


def held_parts(parts, me, w_gate, w_up):
    return hold(
        tuple(GU_PARTS[part] for part in parts),
        tuple(GU_HELD[part] for part in parts),
        me,
        (w_gate, w_up),
    )


def gate_up_kernel(part, n_x, n_before, n_held, me_ref, send_ref, gain_ref, masks, *refs):
    pieces = GU_PARTS[part]
    last = part == GU_LAST
    x_refs, refs = refs[:n_x], refs[n_x:]
    before, refs = refs[: 2 * n_before], refs[2 * n_before :]
    if n_held:
        held, refs = refs[0], refs[1:]
    wg, wu = refs[:2]
    if last:
        out_ref, buf, sem, scaled, acc = refs[2:]
    else:
        acc, sq_ref, buf, sem, scaled = refs[2:]
    rows, cols = scaled.shape[1:]
    depth, hid = wg.shape[1:]
    width = depth // masks.shape[1]
    per = cols // GU_TILE
    kept = GU_TILE // width
    streamed = len(pieces) * per - n_held
    me = me_ref[0]

    def copies(nth, slot):
        row = gate_up_row(me, pieces, cols, n_held + nth)
        return [
            pltpu.make_async_copy(
                w.at[0, pl.ds(row, GU_TILE)], buf.at[slot, j], sem.at[slot, j]
            )
            for j, w in enumerate((wg, wu))
        ]

    slots = min(GU_SLOTS, streamed)
    for nth in range(slots):
        for copy in copies(nth, nth):
            copy.start()
    squares = jnp.zeros((rows, 128), F32)
    at = 0
    for x_ref in x_refs:
        for i in range(x_ref.shape[0]):
            start = pl.multiple_of(place_of(me, pieces[at]) * cols, cols)
            wide = x_ref[i, :, pl.ds(0, cols)].astype(F32)
            for lane in range(0, cols, 128):
                squares = squares + wide[:, lane : lane + 128] * wide[:, lane : lane + 128]
            scaled[at] = (wide * gain_ref[:, pl.ds(start, cols)]).astype(BF)
            at += 1
    if n_before:
        for j in range(2):
            total = before[0][j]
            for i in range(1, n_before):
                total = total + before[2 * i][j]
            acc[j] = total
        for i in range(n_before):
            squares = squares + before[2 * i + 1][...]
    else:
        acc[...] = jnp.zeros_like(acc)

    def add_product(tile, j, weight_ref):
        lanes = pl.ds(pl.multiple_of((tile % per) * GU_TILE, GU_TILE), GU_TILE)
        x_part = scaled[tile // per, :, lanes]
        row = gate_up_row(me, pieces, cols, tile)
        mask = masks[j, pl.ds(pl.multiple_of(row // width, kept), kept), :].astype(BF)
        for start in range(0, hid, GU_SPLIT):
            split = slice(start, start + GU_SPLIT)
            weight = weight_ref[:, split].reshape(kept, width, GU_SPLIT) * mask[:, None, split]
            acc[j, :, split] += jnp.dot(
                x_part, weight.reshape(GU_TILE, GU_SPLIT), preferred_element_type=F32
            )

    def step_body(with_held, nth, carry):
        slot = lax.rem(nth, slots)
        for j, copy in enumerate(copies(nth, slot)):
            if with_held:
                add_product(nth, j, held.at[nth, j])
            copy.wait()
            add_product(n_held + nth, j, buf.at[slot, j])

        @pl.when(nth + slots < streamed)
        def _():
            for copy in copies(nth + slots, slot):
                copy.start()

        return carry

    def held_body(nth, carry):
        for j in range(2):
            add_product(nth, j, held.at[nth, j])
        return carry

    both = min(n_held, streamed)
    if both < n_held:
        lax.fori_loop(both, n_held, held_body, 0)
    if both:
        lax.fori_loop(0, both, functools.partial(step_body, True), 0)
    if both < streamed:
        lax.fori_loop(both, streamed, functools.partial(step_body, False), 0)
    if not last:
        sq_ref[...] = squares
        return
    scale = lax.rsqrt(jnp.sum(squares, axis=1, keepdims=True) / depth + 1e-05)
    gate = acc[0] * scale
    hidden = (gate / (1.0 + jnp.exp(-gate)) * (acc[1] * scale)).astype(BF)
    acc[0] = hidden.astype(F32)

    def load_pair(pair):
        return acc[0, :, pl.ds(pl.multiple_of(pair * 128, 128), 128)]

    each = out_ref.shape[2] // 128
    for piece in range(out_ref.shape[0]):
        for pair in range(each):
            at = piece * 2 * each + 2 * pair
            out_ref[piece, :, pl.ds(pair * 128, 128)] = place(
                load_pair, send_ref[at], send_ref[at + 1]
            )


def gate_up(part, me, send, gain, masks, xs, before, held, w_gate, w_up):
    rows = xs[0].shape[1]
    depth, hid = w_gate.shape[1:]
    cols = depth // 8
    pieces = len(GU_PARTS[part])
    last = part == GU_LAST
    acc = (2, rows, hid)
    scratch = [
        pltpu.VMEM((GU_SLOTS, 2, GU_TILE, hid), BF),
        pltpu.SemaphoreType.DMA((GU_SLOTS, 2)),
        pltpu.VMEM((pieces, rows, cols), BF),
    ]
    if last:
        out_specs, out_shape = VM, jax.ShapeDtypeStruct((8, rows, hid // 8), BF)
        scratch.append(pltpu.VMEM(acc, F32))
    else:
        out_specs = (VM, VM)
        out_shape = (jax.ShapeDtypeStruct(acc, F32), jax.ShapeDtypeStruct((rows, 128), F32))
    operands = list(xs) + list(before) + list(held)
    n_held = held[0].shape[0] if held else 0
    return pl.pallas_call(
        functools.partial(gate_up_kernel, part, len(xs), len(before) // 2, n_held),
        in_specs=[SM, SM, VM, VM] + [VM] * len(operands) + [HB, HB],
        out_specs=out_specs,
        out_shape=out_shape,
        scratch_shapes=scratch,
        compiler_params=pltpu.CompilerParams(vmem_limit_bytes=15 * MIB),
        cost_estimate=pl.CostEstimate(
            flops=4 * rows * pieces * cols * hid,
            bytes_accessed=4 * (pieces * cols - n_held * GU_TILE) * hid,
            transcendentals=0,
        ),
        name="gate_up",
    )(me, send, gain, masks, *operands, w_gate, w_up)


def down_kernel(part, n_held, me_ref, take_ref, inner_ref, x_ref, masks, *refs):
    pieces = DN_PARTS[part]
    if n_held:
        held, refs = refs[0], refs[1:]
    wd, refs = refs[0], refs[1:]
    first, last = part == 0, part == len(DN_PARTS) - 1
    if first:
        out_ref, mine, buf, sem = refs
    elif last:
        out_ref, pass_ref, buf, sem = refs
    else:
        out_ref, buf, sem = refs
    if not first:
        mine = inner_ref
    hid, depth = wd.shape[1:]
    cols = depth // 8
    blocks = masks.shape[1]
    width = hid // blocks
    per = cols // DN_TILE
    streamed = len(pieces) * per - n_held
    n_slots = min(DN_SLOTS, streamed)
    me = me_ref[0]

    def copy_of(nth, slot):
        col = down_col(me, pieces, cols, n_held + nth)
        return pltpu.make_async_copy(wd.at[0, :, pl.ds(col, DN_TILE)], buf.at[slot], sem.at[slot])

    for nth in range(n_slots):
        copy_of(nth, nth).start()
    if first:
        each = inner_ref.shape[2] // 128

        def load_pair(pair):
            lane = pl.multiple_of((pair % each) * 128, 128)
            return inner_ref[pair // each, :, pl.ds(lane, 128)].astype(F32)

        for pair in range(hid // 128):
            mine[:, pl.ds(pair * 128, 128)] = place(
                load_pair, take_ref[2 * pair], take_ref[2 * pair + 1]
            )

    def put(tile, weight_ref):
        mask = masks[down_col(me, pieces, cols, tile) // DN_TILE].astype(BF)
        for start in range(0, DN_TILE, DN_SPLIT):
            split = slice(start, start + DN_SPLIT)
            weight = weight_ref[:, split].reshape(blocks, width, DN_SPLIT) * mask[:, None, split]
            result = jnp.dot(
                mine[...], weight.reshape(hid, DN_SPLIT), preferred_element_type=F32
            )
            lanes = pl.ds(pl.multiple_of((tile % per) * DN_TILE + start, DN_SPLIT), DN_SPLIT)
            out_ref[tile // per, :, lanes] = result.astype(out_ref.dtype)

    def held_body(nth, carry):
        put(nth, held.at[nth])
        return carry

    def step_body(with_held, nth, carry):
        slot = lax.rem(nth, n_slots)
        if with_held:
            put(nth, held.at[nth])
        copy_of(nth, slot).wait()
        put(n_held + nth, buf.at[slot])

        @pl.when(nth + n_slots < streamed)
        def _():
            copy_of(nth + n_slots, slot).start()

        return carry

    both = min(n_held, streamed)
    if both < n_held:
        lax.fori_loop(both, n_held, held_body, 0)
    if both:
        lax.fori_loop(0, both, functools.partial(step_body, True), 0)
    if both < streamed:
        lax.fori_loop(both, streamed, functools.partial(step_body, False), 0)
    if last:
        passed = pass_ref.shape[0]
        pass_ref[...] = out_ref[pl.ds(0, passed)].astype(BF)
        out_ref[passed] += x_ref[:, pl.ds(0, cols)].astype(F32)


def down(part, me, take, inner, x_own, masks, held, w_down):
    hid, depth = w_down.shape[1:]
    rows = x_own.shape[0]
    cols = depth // 8
    pieces = len(DN_PARTS[part])
    n_held = held[0].shape[0] if held else 0
    out = [jax.ShapeDtypeStruct((pieces, rows, cols), F32 if part else BF)]
    if part == 0:
        out.append(jax.ShapeDtypeStruct((rows, hid), BF))
    if part == len(DN_PARTS) - 1:
        out.append(jax.ShapeDtypeStruct((pieces // 2, rows, cols), BF))
    return pl.pallas_call(
        functools.partial(down_kernel, part, n_held),
        in_specs=[SM, SM, VM, VM, VM] + [VM] * len(held) + [HB],
        out_specs=(VM,) * len(out),
        out_shape=tuple(out),
        scratch_shapes=[
            pltpu.VMEM((DN_SLOTS, hid, DN_TILE), BF),
            pltpu.SemaphoreType.DMA((DN_SLOTS,)),
        ],
        compiler_params=pltpu.CompilerParams(vmem_limit_bytes=9 * MIB),
        cost_estimate=pl.CostEstimate(
            flops=2 * rows * pieces * cols * hid,
            bytes_accessed=2 * (pieces * cols - n_held * DN_TILE) * hid,
            transcendentals=0,
        ),
        name="down",
    )(me, take, inner, x_own, masks, *held, w_down)


def partner(block, distance):
    devices = range(lax.axis_size("tp"))
    return lax.ppermute(block, "tp", [(i, i ^ distance) for i in devices])


def onward(block, distance):
    tp_count = lax.axis_size("tp")
    sections = lax.axis_size("section")
    route = [
        (s * tp_count + t, (s + 1) % sections * tp_count + (t ^ distance))
        for s in range(sections)
        for t in range(tp_count)
    ]
    return lax.ppermute(block, ("section", "tp"), route)


def beside_exchanged(blocks):
    chips = blocks.shape[0] // 2
    return jnp.concatenate([blocks[:chips], partner(blocks[chips:], 1)], axis=2)


def along_exchanged(both):
    far_first = [partner(both[k], 2 * k) for k in range(both.shape[0] - 1, 0, -1)]
    return [both[0]] + far_first[::-1]


def sorted_arrivals(got):
    got = jnp.stack(got)
    share = got.shape[2] // 2
    return jnp.concatenate([got[:, :, :share], got[:, :, share:]])


def line_of_eight(
    tokens,
    norm_gain,
    gate_weight,
    up_weight,
    gate_mask,
    up_mask,
    down_weight,
    down_mask,
    slot_order,
):
    sections = lax.axis_size("section")
    tp_count = lax.axis_size("tp")
    section_pos = lax.axis_index("section")
    tp_pos = lax.axis_index("tp")
    rows, cols = tokens.shape
    my_blocks = slot_order[0]
    per_device = my_blocks.shape[0]
    chips = tp_count // 2
    me = tp_pos.astype(jnp.int32).reshape(1)

    gate_weight, up_weight, down_weight = (
        pltpu.with_memory_space_constraint(w, pltpu.HBM)
        for w in (gate_weight, up_weight, down_weight)
    )
    numbers = jnp.pad(my_blocks, (0, 128 - per_device)).astype(BF)
    own = jnp.concatenate([tokens, jnp.broadcast_to(numbers[None], (rows, 128))], axis=1)
    send = jnp.zeros((per_device,), jnp.int32)
    gu_masks, dn_masks, norm_gain = spread_masks(
        gate_mask[0].T,
        up_mask[0].T,
        down_mask[0],
        norm_gain,
        gate_weight.shape[2],
        down_weight.shape[2],
    )
    gu_held = [[]] * len(GU_HELD)
    saved = jnp.zeros(tokens.shape, BF)
    for round_pos in range(sections):
        straight = [partner(own, 2 * k) for k in range(chips - 1, 0, -1)]
        beside = partner(own, 1)
        arrivals = gate_up(
            0, me, send, norm_gain, gu_masks, [own[None], beside[None]], [], gu_held[0],
            gate_weight, up_weight,
        )
        if round_pos:
            straight[0], arrivals = lax.optimization_barrier((straight[0], arrivals))
            arrivals = gate_up(
                1, me, send, norm_gain, gu_masks, [straight[0][None]], arrivals, gu_held[1],
                gate_weight, up_weight,
            )
        straight, arrivals = lax.optimization_barrier((straight, arrivals))
        near = jnp.stack(straight)
        far = partner(near, 1)
        part = 2 if round_pos else GU_FIRST_ROUND
        arrivals = gate_up(
            part, me, send, norm_gain, gu_masks,
            [x[None] for x in straight[-len(GU_PARTS[part]) :]], arrivals,
            gu_held[part], gate_weight, up_weight,
        )
        far, arrivals = lax.optimization_barrier((far, arrivals))
        if round_pos == 0:
            send, take = slots(
                me, [own[None], near, beside[None], far], ((0,), (3, 2, 1), (4,), (7, 6, 5)),
                cols, per_device,
            )
        blocks = gate_up(
            3, me, send, norm_gain, gu_masks, [far], arrivals, gu_held[3],
            gate_weight, up_weight,
        )
        both, turn = lax.optimization_barrier((beside_exchanged(blocks), me))
        parts = [part for part, count in enumerate(DN_HELD) if count]
        tiles = hold(
            tuple(DN_PARTS[part] for part in parts),
            tuple(DN_HELD[part] for part in parts),
            turn,
            (down_weight,),
        )
        got, tiles = lax.optimization_barrier((along_exchanged(both), tiles))
        dn_held = [[]] * len(DN_HELD)
        for part, held in zip(parts, tiles):
            dn_held[part] = [held]
        arrived = sorted_arrivals(got)
        passed, mine = down(0, me, take, arrived, own, dn_masks, dn_held[0], down_weight)
        got = partner(passed, 1).astype(F32)
        (kept,) = down(1, me, take, mine, own, dn_masks, dn_held[1], down_weight)
        outward, mine = lax.optimization_barrier(((kept + got).astype(BF), mine))
        nearer = partner(outward, 2)
        kept, passed = down(2, me, take, mine, own, dn_masks, dn_held[2], down_weight)
        nearer, kept, passed = lax.optimization_barrier((nearer, kept, passed))
        sums = kept[2:] + partner(passed, 1).astype(F32) + nearer.astype(F32)
        sums = sums.astype(BF)
        sums, turn = lax.optimization_barrier((sums, me))
        parts = GU_BROUGHT if round_pos else GU_BROUGHT + GU_STAYING
        far_half = onward(sums[1], 4)
        halves = [far_half, onward(sums[0], 0)]
        if round_pos + 1 < sections:
            tiles = held_parts(parts, turn, gate_weight, up_weight)
            halves, tiles = lax.optimization_barrier((halves, tiles))
            for part, held in zip(parts, tiles):
                gu_held[part] = [held]
        own = (halves[0].astype(F32) + halves[1].astype(F32)).astype(BF)
        saved = jnp.where(section_pos == (round_pos + 1) % sections, own, saved)
    return saved[None]


def solution(mesh):
    tp_count = mesh.shape["tp"]
    line_body = line_of_eight if tp_count == 8 else ring_body
    return jax.shard_map(
        line_body,
        mesh=mesh,
        in_specs=(
            P(None, "tp"),
            P("section", None),
            P("section", None, "tp"),
            P("section", None, "tp"),
            P("section", None, "tp"),
            P("section", None, "tp"),
            P("section", "tp", None),
            P("section", "tp", None),
            P("section", "tp"),
        ),
        out_specs=P("section", None, "tp"),
        check_vma=False,
    )
```
